128 devices in a mesh: row: 8 (over x_lo, y), col: 16 (over z, x_hi, core).
Axes of the slice: x: 4 (x_hi: 2, x_lo: 2; x = x_hi * 2 + x_lo), y: 4, z: 4, core: 2. Of those that a mesh axis runs over, the one named last changes fastest.
Arguments:
- pair: bfloat16 [512, 512, 128], P('row', 'col'), may hold values from -6 to 6
- chain_id: int32 [512], replicated, may hold values from 0 to 3, never falling along the last dimension, each value on 1 to 256 neighbouring positions
- block_mask: int32 [8, 8], replicated, may hold values 0 or 1
- norm_gains: float32 [5, 128], replicated, may hold values from 0.1 to 1.9
- mult_in_weights: bfloat16 [2, 128, 640], replicated, may hold values from -0.5 to 0.5
- mult_out_weights: bfloat16 [2, 128, 128], replicated, may hold values from -0.5 to 0.5
- attn_weights: bfloat16 [128, 512], replicated, may hold values from -0.5 to 0.5
- bias_weights: bfloat16 [128, 4], replicated, may hold values from -0.5 to 0.5
- attn_out_weights: bfloat16 [128, 128], replicated, may hold values from -0.5 to 0.5
Outputs:
- pair_out: bfloat16 [512, 512, 128], P('row', 'col')
The draws below stay inside these ranges and needn't reach their ends.
Inputs may be any that keep to these rules, and one draw needn't show every extreme that they name: `chain_id`: chains are runs of consecutive tokens; one chain holds exactly 256 tokens.
All inputs are finite; a program needn't handle non-finite values.
Results may differ from the reference program's by a relative error of at most 0.025.
Values may be sent and summed in bfloat16 or wider, within the bound.
A program may use at most 128 MiB of HBM per device.

```python
import math
import jax
import jax.numpy as jnp
import numpy as np
from jax import lax

C = 128
H = 4
BLK = 64
CHAINS = 4
N = 512
NB = 8
N_ROW = 8
N_COL = 16


def with_ends(array, own_key, smallest, top_value):
    dims = array.shape
    index_at = [jax.random.randint(jax.random.fold_in(own_key, axis), (), 0, dims[axis]) for axis in range(len(dims))]
    array = array.at[tuple(index_at)].set(smallest)
    longest = dims.index(max(dims))
    index_at[longest] = (index_at[longest] + 1) % dims[longest]
    return array.at[tuple(index_at)].set(top_value)


def level_of(own_key, dims, cuts, smallest, top_value):
    loudness, own = 1.0, jax.random.fold_in(own_key, 6)
    for axis_at, shards_of in cuts:
        heights = jnp.exp(jax.random.uniform(jax.random.fold_in(own, axis_at), (shards_of,), jnp.float32, smallest / len(cuts), top_value / len(cuts)))
        loudness = loudness * jnp.repeat(heights, dims[axis_at] // shards_of).reshape([-1 if axis == axis_at else 1 for axis in range(len(dims))])
    return loudness


def split_up(count, total, reach, lean):
    loads = [(1 << 20) // math.isqrt(rank ** lean) + 1 for rank in range(2, count + 1)]
    surplus, counts = total - reach - (count - 1), [1] * (count - 1)
    while surplus > 0:
        candidates = [i for i in range(count - 1) if counts[i] < reach]
        mass, remaining = sum([loads[i] for i in candidates]), surplus
        for i in candidates:
            addition = min(reach - counts[i], max(1, remaining * loads[i] // mass), surplus)
            counts[i] = counts[i] + addition
            surplus = surplus - addition
    return np.array([reach] + counts)


def ragged(own_key, amount, total, limit, slope):
    if amount == 2:
        one = jax.random.randint(own_key, (), max(1, total - limit), min(limit, total - 1) + 1)
        return jnp.stack([one, total - one])
    sizes = jnp.asarray(split_up(amount, total, limit, slope), jnp.int32)
    couples = (amount - 1) // 2
    giver, sink = sizes[1:1 + 2 * couples:2], sizes[2:2 + 2 * couples:2]
    slack = jnp.minimum(giver - 1, limit - sink)
    shifted = jax.random.randint(jax.random.fold_in(own_key, 1), (couples,), 0, 1 << 20) % (slack + 1)
    sizes = sizes.at[1:1 + 2 * couples:2].set(giver - shifted).at[2:2 + 2 * couples:2].set(sink + shifted)
    return sizes[jax.random.permutation(jax.random.fold_in(own_key, 2), amount)]


def normal_values(stream_key, dims, scale, bound, pieces=(), kind=jnp.bfloat16):
    factor_of = level_of(stream_key, dims, pieces, -0.22, 0.18) if pieces else 1.0
    values = jax.random.normal(stream_key, dims, jnp.float32) * scale * factor_of
    return jnp.minimum(jnp.maximum(values, -bound), bound).astype(kind)


def setup_inputs(seed: int = 0) -> dict:
    arg_keys = jax.random.split(jax.random.key(seed), 10)
    return {
        "pair": normal_values(arg_keys[0], (N, N, C), 1.0, 6.0, ((0, 8), (1, 16))),
        "chain_id": jnp.searchsorted(jnp.cumsum(ragged(arg_keys[1], CHAINS, N, N // 2, 2)), jnp.arange(N), side="right").astype(jnp.int32),
        "block_mask": with_ends((jax.random.randint(arg_keys[2], (NB, NB), 0, 2) < 1).astype(jnp.int32), jax.random.fold_in(arg_keys[2], 1), 0, 1),
        "norm_gains": jnp.clip(1.0 + 0.18 * jax.random.normal(arg_keys[3], (5, C), jnp.float32), 0.1, 1.9),
        "mult_in_weights": normal_values(arg_keys[4], (2, C, 5 * C), C ** -0.5, 0.5),
        "mult_out_weights": normal_values(arg_keys[5], (2, C, C), C ** -0.5, 0.5),
        "attn_weights": normal_values(arg_keys[6], (C, 4 * C), C ** -0.5, 0.5),
        "bias_weights": normal_values(arg_keys[7], (C, H), C ** -0.5, 0.5),
        "attn_out_weights": normal_values(arg_keys[8], (C, C), C ** -0.5, 0.5),
    }


def layer_norm(values, gain):
    center = values - lax.optimization_barrier(jnp.mean(values, axis=-1, keepdims=True))
    spread = lax.optimization_barrier(jnp.mean(center * center, axis=-1, keepdims=True))
    return center * lax.rsqrt(spread + 1e-05) * gain

def allowed_pairs(chain_id, block_mask, row_first, row_count, col_first, col_count, block_size):
    row_chain = lax.dynamic_slice_in_dim(chain_id, row_first, row_count)
    col_chain = lax.dynamic_slice_in_dim(chain_id, col_first, col_count)
    same_chain = row_chain[:, None] == col_chain[None, :]
    blocks = block_mask.shape[0]
    block_ids = jnp.arange(blocks, dtype=jnp.int32)
    row_block = (row_first + jnp.arange(row_count, dtype=jnp.int32)) // block_size
    col_block = (col_first + jnp.arange(col_count, dtype=jnp.int32)) // block_size
    row_onehot = (row_block[:, None] == block_ids[None, :]).astype(jnp.float32)
    col_onehot = (col_block[:, None] == block_ids[None, :]).astype(jnp.float32)
    lookup = jnp.dot(jnp.dot(row_onehot, block_mask.astype(jnp.float32)), col_onehot.T)
    return jnp.logical_or(same_chain, lookup > 0.5)

def tri_gates(pair, gain_in, weights_in, allowed):
    channels = pair.shape[-1]
    normed = layer_norm(pair.astype(jnp.float32), gain_in).astype(jnp.bfloat16)
    projected = jnp.dot(normed, weights_in, preferred_element_type=jnp.float32)
    keep = allowed.astype(jnp.float32)[..., None]
    left_edge = (jax.nn.sigmoid(projected[..., :channels]) * projected[..., channels:2 * channels] * keep).astype(jnp.bfloat16)
    right_edge = (jax.nn.sigmoid(projected[..., 2 * channels:3 * channels]) * projected[..., 3 * channels:4 * channels] * keep).astype(jnp.bfloat16)
    gating = jax.nn.sigmoid(projected[..., 4 * channels:])
    return (left_edge, right_edge, gating)

def tri_finish(pair, combined, gain_out, weight_out, gating):
    normed = layer_norm(combined, gain_out).astype(jnp.bfloat16)
    update = gating * jnp.dot(normed, weight_out, preferred_element_type=jnp.float32)
    return (pair.astype(jnp.float32) + update).astype(jnp.bfloat16)

def grouped_sum(left_edge, right_edge, groups, axis_k, form):
    extent = left_edge.shape[0]
    group_width = extent // groups

    def add_group(running, group_index):
        left_part = lax.dynamic_slice_in_dim(left_edge, group_index * group_width, group_width, axis_k).astype(jnp.float32)
        right_part = lax.dynamic_slice_in_dim(right_edge, group_index * group_width, group_width, axis_k).astype(jnp.float32)
        partial_sum = jnp.einsum(form, left_part, right_part)
        rounded = lax.optimization_barrier(partial_sum.astype(jnp.bfloat16)).astype(jnp.float32)
        return (running + rounded, None)
    start_value = jnp.zeros(left_edge.shape, jnp.float32)
    running, _ = lax.scan(add_group, start_value, jnp.arange(groups, dtype=jnp.int32))
    return running

def attend(pair, gain, attn_weights, bias_weights, out_weights, allowed):
    extent, _, channels = pair.shape
    head_count = bias_weights.shape[1]
    head_dim = channels // head_count
    normed = layer_norm(pair.astype(jnp.float32), gain).astype(jnp.bfloat16)
    projected = jnp.dot(normed, attn_weights, preferred_element_type=jnp.float32)
    queries = (projected[..., :channels] * head_dim ** (-0.5)).astype(jnp.bfloat16)
    key_rows = projected[..., channels:2 * channels].astype(jnp.bfloat16)
    value_rows = projected[..., 2 * channels:3 * channels].astype(jnp.bfloat16)
    gating = jax.nn.sigmoid(projected[..., 3 * channels:])
    pair_bias = jnp.dot(normed, bias_weights, preferred_element_type=jnp.float32).astype(jnp.bfloat16)
    bias_heads = jnp.transpose(pair_bias, (2, 0, 1)).astype(jnp.float32)
    penalty = jnp.where(allowed, 0.0, -1000000000.0).astype(jnp.float32)
    rows_block = math.gcd(extent, 32)
    block_count = extent // rows_block

    def one_block(block_index):
        row_first = block_index * rows_block
        query_part = lax.dynamic_slice_in_dim(queries, row_first, rows_block, 0).reshape(rows_block, extent, head_count, head_dim).astype(jnp.float32)
        key_part = lax.dynamic_slice_in_dim(key_rows, row_first, rows_block, 0).reshape(rows_block, extent, head_count, head_dim).astype(jnp.float32)
        value_part = lax.dynamic_slice_in_dim(value_rows, row_first, rows_block, 0).reshape(rows_block, extent, head_count, head_dim).astype(jnp.float32)
        penalty_part = lax.dynamic_slice_in_dim(penalty, row_first, rows_block, 0)
        scores = jnp.einsum('ijhd,ikhd->ihjk', query_part, key_part) + bias_heads[None] + penalty_part[:, None, None, :]
        raised = jnp.exp(scores)
        shares = (raised / lax.optimization_barrier(jnp.sum(raised, axis=-1, keepdims=True))).astype(jnp.bfloat16)
        mixed = jnp.einsum('ihjk,ikhd->ijhd', shares.astype(jnp.float32), value_part).reshape(rows_block, extent, channels)
        gating_part = lax.dynamic_slice_in_dim(gating, row_first, rows_block, 0)
        gated = (gating_part * mixed).astype(jnp.bfloat16)
        pair_part = lax.dynamic_slice_in_dim(pair, row_first, rows_block, 0).astype(jnp.float32)
        return (pair_part + jnp.dot(gated, out_weights, preferred_element_type=jnp.float32)).astype(jnp.bfloat16)
    blocks = lax.map(one_block, jnp.arange(block_count, dtype=jnp.int32))
    return blocks.reshape(extent, extent, channels)

def reference(pair, chain_id, block_mask, norm_gains, mult_in_weights, mult_out_weights, attn_weights, bias_weights, attn_out_weights):
    extent = pair.shape[0]
    allowed = allowed_pairs(chain_id, block_mask, 0, extent, 0, extent, BLK)
    left_edge, right_edge, gating = tri_gates(pair, norm_gains[0], mult_in_weights[0], allowed)
    combined = grouped_sum(left_edge, right_edge, N_COL, 1, 'ikc,jkc->ijc')
    pair_one = tri_finish(pair, combined, norm_gains[1], mult_out_weights[0], gating)
    left_edge, right_edge, gating = tri_gates(pair_one, norm_gains[2], mult_in_weights[1], allowed)
    combined = grouped_sum(left_edge, right_edge, N_ROW, 0, 'kic,kjc->ijc')
    pair_two = tri_finish(pair_one, combined, norm_gains[3], mult_out_weights[1], gating)
    return attend(pair_two, norm_gains[4], attn_weights, bias_weights, attn_out_weights, allowed)
```

```python
import functools

import jax
import jax.numpy as jnp
from jax import lax
from jax.experimental import pallas as pl
from jax.experimental.pallas import tpu as pltpu
from jax.sharding import PartitionSpec as P

MESH = pl.DeviceIdType.MESH
F32 = jnp.float32
BF16 = jnp.bfloat16
ROWS = 8
COLS = 16
DEV = ROWS * COLS
C = 128
N = 512
H = 4
OWN = 4


def dot(a, b):
    return jnp.dot(a, b, preferred_element_type=F32)


def dot_nt(a, b):
    return lax.dot_general(a, b, (((1,), (1,)), ((), ())), preferred_element_type=F32)


def norm_cm(x, gain):
    center = x - jnp.mean(x, axis=0, keepdims=True)
    spread = jnp.mean(center * center, axis=0, keepdims=True)
    return center * lax.rsqrt(spread + 1e-05) * gain


def kernel(
    pair,
    chain_s,
    chain_v,
    block_s,
    gains,
    w_in,
    w_out,
    w_attn,
    w_bias,
    w_final,
    out,
    rows_in,
    pair_cm,
    gate_cm,
    norm_c,
    keep,
    gain_b,
    wt_in,
    wt_out,
    wt_k,
    wt_bias,
    wide,
    edges,
    send_a,
    recv_a,
    send_b,
    recv_b,
    bias_send,
    bias_recv,
    bias_wide,
    bias_nat,
    q_ext,
    k_ext,
    v_ext,
    rows_out,
    sem_send,
    sem_recv,
):
    r = lax.axis_index("row")
    c = lax.axis_index("col")
    me = r * COLS + c

    def device(t):
        return (lax.div(t, COLS), lax.rem(t, COLS))

    barrier = pltpu.get_barrier_semaphore()

    @pl.loop(1, DEV)
    def _(step):
        pl.semaphore_signal(
            barrier, inc=1, device_id=device(lax.rem(me + step, DEV)), device_id_type=MESH
        )

    for n in range(5):
        gain_b[n] = jnp.transpose(jnp.broadcast_to(gains[n : n + 1, :], (C, C)))
    for t in range(2):
        for g in range(5):
            part = w_in[t, :, g * C : (g + 1) * C].astype(F32)
            wt_in[t, g * C : (g + 1) * C, :] = jnp.transpose(part).astype(BF16)
        wt_out[t] = jnp.transpose(w_out[t].astype(F32)).astype(BF16)
    wt_k[...] = jnp.transpose(w_attn[:, C : 2 * C].astype(F32)).astype(BF16)
    wt_bias[...] = jnp.transpose(w_bias[...].astype(F32)).astype(BF16)
    block_of = lax.broadcasted_iota(jnp.int32, (1, N), 1) // 64
    linked = jnp.zeros((1, N), jnp.int32)
    for nb in range(8):
        linked = jnp.where(block_of == nb, block_s[r, nb], linked)
    for a in range(OWN):
        own_chain = chain_s[r * 64 + a * 16 + c]
        allowed = jnp.logical_or(chain_v[...] == own_chain, linked == 1)
        keep[a : a + 1, :] = jnp.where(allowed, 1.0, 0.0).astype(F32)

    pl.semaphore_wait(barrier, DEV - 1)

    pltpu.make_async_copy(
        pair.at[:, c], rows_in.at[:, pl.ds(c * 32, 32)], sem_recv.at[0]
    ).start()

    @pl.loop(1, COLS)
    def _(step):
        t = lax.rem(c + step, COLS)
        pltpu.make_async_remote_copy(
            pair.at[:, t],
            rows_in.at[:, pl.ds(c * 32, 32)],
            sem_send.at[0],
            sem_recv.at[0],
            device_id=(r, t),
            device_id_type=MESH,
        ).start()

    pltpu.make_async_copy(rows_in, rows_in, sem_recv.at[0]).wait()

    @pl.loop(0, OWN)
    def _(a):
        x = jnp.transpose(rows_in[a].astype(F32))
        pair_cm[a] = x
        norm_c[a] = norm_cm(x, jnp.tile(gain_b[0], (1, 4))).astype(BF16)

    def send_chunk(source, target, t, k):
        @pl.when(t == me)
        def _():
            pltpu.make_async_copy(source.at[t], target.at[me], sem_recv.at[k]).start()

        @pl.when(t != me)
        def _():
            pltpu.make_async_remote_copy(
                source.at[t],
                target.at[me],
                sem_send.at[k],
                sem_recv.at[k],
                device_id=device(t),
                device_id_type=MESH,
            ).start()

    def send_edges(t, k):
        @pl.loop(0, 4)
        def _(step):
            base = pl.multiple_of(lax.rem(lax.div(me, 32) + step, 4) * 32, 32)
            for a in range(OWN):
                x = norm_c[a]
                mask = keep[a : a + 1, :]
                for side in range(2):
                    g = dot(wt_in[t, pl.ds(2 * side * C + base, 32), :], x)
                    v = dot(wt_in[t, pl.ds((2 * side + 1) * C + base, 32), :], x)
                    e = jax.nn.sigmoid(g) * v * mask
                    for b in range(4):
                        wide[pl.ds(base * 32 + side * 16 + a * 4 + b, 32, stride=32), :] = e[
                            :, b * 128 : (b + 1) * 128
                        ]
            part = wide[pl.ds(pl.multiple_of(base * 32, 1024), 1024), :]
            send_a[t, pl.ds(base, 32)] = part.reshape(32, 32, 128).astype(BF16)

            @pl.loop(0, 32)
            def _(s):
                send_chunk(send_a.at[t], recv_a.at[t], base + lax.rem(me + s, 32), k)

        for a in range(OWN):
            gate_cm[a] = jax.nn.sigmoid(dot(wt_in[t, 4 * C : 5 * C, :], norm_c[a]))

    def triangle(t, k):
        pltpu.make_async_copy(recv_a.at[t], recv_a.at[t], sem_recv.at[k]).wait()

        @pl.loop(0, ROWS)
        def _(q):
            first = pl.multiple_of(q * 512, 512)
            wide[pl.ds(first, 512), :] = (
                recv_a[t, pl.ds(q * 16, 16)].astype(F32).reshape(512, 128)
            )
            for side in range(2):
                for a in range(OWN):
                    for b in range(4):
                        block = wide[pl.ds(first + side * 16 + a * 4 + b, 16, stride=32), :]
                        edges[
                            side, pl.ds(q * 64 + a * 16, 16), b * 128 : (b + 1) * 128
                        ] = block.astype(BF16)

        @pl.loop(0, 4)
        def _(step):
            q = lax.rem(lax.div(me, 32) + step, 4)
            if t == 0:
                left = edges[0, pl.ds(pl.multiple_of(q * 128, 128), 128), :]
                total = dot_nt(left, edges[1])
            else:
                left = edges[0, :, pl.ds(pl.multiple_of(q * 128, 128), 128)]
                total = dot(jnp.transpose(left.astype(F32)).astype(BF16), edges[1])
            for half in range(2):
                for a in range(OWN):
                    for b in range(4):
                        wide[
                            pl.ds(q * 512 + half * 256 + a * 4 + b, 16, stride=16), :
                        ] = total[
                            half * 64 + a * 16 : half * 64 + a * 16 + 16,
                            b * 128 : (b + 1) * 128,
                        ]
            part = wide[pl.ds(pl.multiple_of(q * 512, 512), 512), :]
            send_b[t, pl.ds(q * 32, 32)] = part.reshape(32, 16, 128).astype(BF16)

            @pl.loop(0, 32)
            def _(s):
                send_chunk(send_b.at[t], recv_b.at[t], q * 32 + lax.rem(me + s, 32), k + 1)

    def finish(t, k, then):
        pltpu.make_async_copy(recv_b.at[t], recv_b.at[t], sem_recv.at[k]).wait()
        wide[0:2048, :] = recv_b[t].astype(F32).reshape(2048, 128)

        @pl.loop(0, OWN)
        def _(a):
            total = jnp.concatenate(
                [wide[pl.ds(a * 4 + b, 128, stride=16), :] for b in range(4)], axis=1
            )
            normed = norm_cm(total, jnp.tile(gain_b[2 * t + 1], (1, 4))).astype(BF16)
            update = gate_cm[a] * dot(wt_out[t], normed)
            new = (pair_cm[a] + update).astype(BF16).astype(F32)
            pair_cm[a] = new
            then(a, norm_cm(new, jnp.tile(gain_b[2 * t + 2], (1, 4))))

    send_edges(0, 1)
    triangle(0, 1)

    def keep_norm(a, normed):
        norm_c[a] = normed.astype(BF16)

    finish(0, 2, keep_norm)
    send_edges(1, 3)
    triangle(1, 3)

    def bias_part(a, normed):
        rounded = normed.astype(BF16)
        norm_c[a] = rounded
        bias = dot(wt_bias[...], rounded)
        for kb in range(4):
            bias_wide[pl.ds(kb * 16 + a, 4, stride=4), :] = bias[
                0:H, kb * 128 : (kb + 1) * 128
            ]

    finish(1, 4, bias_part)
    bias_send[...] = bias_wide[0:64, :].reshape(4, 16, 128).astype(BF16)

    pltpu.make_async_copy(bias_send, bias_recv.at[me], sem_recv.at[5]).start()

    @pl.loop(1, DEV)
    def _(step):
        pltpu.make_async_remote_copy(
            bias_send,
            bias_recv.at[me],
            sem_send.at[5],
            sem_recv.at[5],
            device_id=device(lax.rem(me + step, DEV)),
            device_id_type=MESH,
        ).start()

    lane = lax.broadcasted_iota(jnp.int32, (N, C), 1)
    first_row = lax.broadcasted_iota(jnp.int32, (C, N), 0) == 0
    q_ext[:, :, C:] = jnp.where(lane == 0, 1.0, 0.0).astype(BF16)[None] * jnp.ones(
        (OWN, 1, 1), BF16
    )
    v_ext[:, C:] = jnp.ones((N, C), BF16)

    @pl.loop(0, OWN)
    def _(a):
        k_ext[a, 0:C, :] = dot(wt_k[...], norm_c[a]).astype(BF16)
        penalty = jnp.where(keep[pl.ds(a, 1), :] > 0.5, 0.0, -1e9)
        k_ext[a, C:, :] = jnp.where(first_row, penalty, 0.0).astype(BF16)
        rows = jnp.transpose(norm_c[a].astype(F32)).astype(BF16)
        rows_in[a] = rows
        q_ext[a, :, 0:C] = (dot(rows, w_attn[:, 0:C]) * 32**-0.5).astype(BF16)

    pltpu.make_async_copy(bias_recv, bias_recv, sem_recv.at[5]).wait()

    @pl.loop(0, ROWS)
    def _(q):
        bias_wide[...] = bias_recv[pl.ds(q * 16, 16)].astype(F32).reshape(1024, 128)
        for h in range(H):
            for a in range(OWN):
                for kb in range(4):
                    bias_nat[
                        h, pl.ds(q * 64 + a * 16, 16), kb * 128 : (kb + 1) * 128
                    ] = bias_wide[pl.ds(kb * 16 + h * 4 + a, 16, stride=64), :]

    @pl.loop(0, OWN)
    def _(a):
        rows = rows_in[a]
        values = dot(rows, w_attn[:, 2 * C : 3 * C])
        total = jnp.zeros((N, C), F32)
        for h in range(H):
            here = jnp.logical_and(lane >= 32 * h, lane < 32 * (h + 1))
            v_ext[:, 0:C] = jnp.where(here, values, 0.0).astype(BF16)
            lane2 = lax.broadcasted_iota(jnp.int32, (N, 2 * C), 1)
            here2 = jnp.logical_or(
                jnp.logical_and(lane2 >= 32 * h, lane2 < 32 * (h + 1)), lane2 >= C
            )
            query = jnp.where(here2, q_ext[a].astype(F32), 0.0).astype(BF16)
            scores = dot(query, k_ext[a]) + bias_nat[h]
            raised = jnp.exp(scores).astype(BF16)
            mixed = dot(raised, v_ext[...])
            total = total + mixed[:, 0:C] / mixed[:, C:]
        gating = jax.nn.sigmoid(dot(rows, w_attn[:, 3 * C :]))
        gated = (gating * total).astype(BF16)
        update = dot(gated, w_final[...])
        rows_out[a] = (jnp.transpose(pair_cm[a]) + update).astype(BF16)

    pltpu.make_async_copy(
        rows_out.at[:, pl.ds(c * 32, 32)], out.at[:, c], sem_recv.at[6]
    ).start()

    @pl.loop(1, COLS)
    def _(step):
        t = lax.rem(c + step, COLS)
        pltpu.make_async_remote_copy(
            rows_out.at[:, pl.ds(t * 32, 32)],
            out.at[:, c],
            sem_send.at[6],
            sem_recv.at[6],
            device_id=(r, t),
            device_id_type=MESH,
        ).start()

    pltpu.make_async_copy(out, out, sem_recv.at[6]).wait()

    def sent(array, k):
        pltpu.make_async_copy(array, array, sem_send.at[k]).wait()

    sent(out.at[:, pl.ds(0, COLS - 1)], 0)
    sent(out.at[:, pl.ds(0, COLS - 1)], 6)
    for t in range(2):
        sent(recv_a.at[t, pl.ds(0, DEV - 1)], 2 * t + 1)
        sent(recv_b.at[t, pl.ds(0, DEV - 1)], 2 * t + 2)
    sent(bias_recv.at[pl.ds(0, DEV - 1)], 5)


def per_device(
    pair, chain_id, block_mask, norm_gains, w_in, w_out, w_attn, w_bias, w_final
):
    vmem = pl.BlockSpec(memory_space=pltpu.VMEM)
    smem = pl.BlockSpec(memory_space=pltpu.SMEM)
    result = pl.pallas_call(
        kernel,
        out_shape=jax.ShapeDtypeStruct((OWN, COLS, 32, C), BF16),
        in_specs=[vmem, smem, vmem, smem] + [vmem] * 6,
        out_specs=vmem,
        scratch_shapes=[
            pltpu.VMEM((OWN, N, C), BF16),
            pltpu.VMEM((OWN, C, N), F32),
            pltpu.VMEM((OWN, C, N), F32),
            pltpu.VMEM((OWN, C, N), BF16),
            pltpu.VMEM((8, N), F32),
            pltpu.VMEM((5, C, C), F32),
            pltpu.VMEM((2, 5 * C, C), BF16),
            pltpu.VMEM((2, C, C), BF16),
            pltpu.VMEM((C, C), BF16),
            pltpu.VMEM((16, C), BF16),
            pltpu.VMEM((4096, C), F32),
            pltpu.VMEM((2, N, N), BF16),
            pltpu.VMEM((2, DEV, 32, C), BF16),
            pltpu.VMEM((2, DEV, 32, C), BF16),
            pltpu.VMEM((2, DEV, 16, C), BF16),
            pltpu.VMEM((2, DEV, 16, C), BF16),
            pltpu.VMEM((4, 16, C), BF16),
            pltpu.VMEM((DEV, 4, 16, C), BF16),
            pltpu.VMEM((1024, C), F32),
            pltpu.VMEM((H, N, N), F32),
            pltpu.VMEM((OWN, N, 2 * C), BF16),
            pltpu.VMEM((OWN, 2 * C, N), BF16),
            pltpu.VMEM((N, 2 * C), BF16),
            pltpu.VMEM((OWN, N, C), BF16),
            pltpu.SemaphoreType.DMA((7,)),
            pltpu.SemaphoreType.DMA((7,)),
        ],
        name="triangle_block",
        compiler_params=pltpu.CompilerParams(
            collective_id=0, has_side_effects=True, vmem_limit_bytes=56 << 20
        ),
        cost_estimate=pl.CostEstimate(
            flops=3 * 10**9, bytes_accessed=2 * 10**6, transcendentals=5 * 10**6
        ),
    )(
        pair.reshape(OWN, COLS, 32, C),
        chain_id,
        chain_id.reshape(1, N),
        block_mask,
        norm_gains,
        w_in,
        w_out,
        w_attn,
        jnp.pad(w_bias, ((0, 0), (0, 12))),
        w_final,
    )
    return result.reshape(64, 32, C)


def solution(mesh):
    placed = (P("row", "col", None), P(), P(), P(), P(), P(), P(), P(), P())
    return jax.shard_map(
        per_device, mesh=mesh, in_specs=placed, out_specs=P("row", "col", None), check_vma=False
    )
```

```python
import jax
import jax.numpy as jnp
from jax import lax
from jax.experimental import pallas as pl
from jax.experimental.pallas import tpu as pltpu
from jax.sharding import PartitionSpec as P

MESH = pl.DeviceIdType.MESH
F32 = jnp.float32
BF16 = jnp.bfloat16
ROWS = 8
COLS = 16
DEV = ROWS * COLS
CHIPS = DEV // 2
C = 128
N = 512
HALF = N // 2
H = 4
OWN = 4
LOG2E = 1.4426950408889634

FAR = (
    (699248298, 5),
    (791255470, 5),
    (966748069, 5),
    (770581915, 5),
    (199256638, 5),
    (744454258, 5),
    (160421045, 5),
    (612196317, 5),
    (322204568, 5),
    (336278469, 5),
    (539184252, 5),
    (51578641, 5),
    (49232, 3),
)


def dot(a, b):
    return jnp.dot(a, b, preferred_element_type=F32)


def norm_cm(x, gain):
    center = x - jnp.mean(x, axis=0, keepdims=True)
    spread = jnp.mean(center * center, axis=0, keepdims=True)
    return center * lax.rsqrt(spread + 1e-05) * gain


def kernel(
    pair,
    chain_s,
    chain_v,
    block_s,
    gains,
    w_in,
    w_out,
    w_attn,
    w_bias,
    w_final,
    out,
    rows_in,
    pair_cm,
    gate_cm,
    norm8,
    norm_0,
    keep8,
    keep_0,
    gain_b,
    wt_in,
    wt_out,
    wt_k,
    wide,
    edges,
    send_a,
    recv_a,
    send_b,
    recv_b,
    bias_send,
    bias_recv,
    bias_nat,
    half_send,
    resid8,
    q_ext,
    k_ext,
    v_ext,
    gate8,
    total8,
    rows_out,
    sem_send,
    sem_recv,
):
    r = lax.axis_index("row")
    c = lax.axis_index("col")
    core = lax.rem(c, 2)
    duo = lax.div(c, 2)
    chip = r * 8 + duo
    me = core * CHIPS + chip
    place = core * 8 + duo
    other = 1 - core
    cx = lax.rem(duo, 2) * 2 + lax.div(r, 4)
    cy = lax.rem(r, 4)
    cz = lax.div(duo, 2)

    barrier = pltpu.get_barrier_semaphore()

    @pl.loop(1, DEV)
    def _(step):
        t = lax.rem(r * COLS + c + step, DEV)
        pl.semaphore_signal(
            barrier, inc=1, device_id=(lax.div(t, COLS), lax.rem(t, COLS)), device_id_type=MESH
        )

    def far_chips(visit):
        for packed, count in FAR:

            def body(_, value):
                d = lax.rem(value, 64)
                x = lax.rem(cx + lax.rem(d, 4), 4)
                y = lax.rem(cy + lax.rem(lax.div(d, 4), 4), 4)
                z = lax.rem(cz + lax.div(d, 16), 4)
                visit(lax.rem(x, 2) * 4 + y, z * 2 + lax.div(x, 2))
                return lax.div(value, 64)

            lax.fori_loop(0, count, body, jnp.int32(packed))

    def chunk(source, target, k, r2, duo2, core2):
        t = core2 * CHIPS + r2 * 8 + duo2
        pltpu.make_async_remote_copy(
            source.at[t],
            target.at[me],
            sem_send.at[k],
            sem_recv.at[k],
            device_id=(r2, duo2 * 2 + core2),
            device_id_type=MESH,
        ).start()

    def send_far(source, target, k, cores):
        def visit(r2, duo2):
            for core2 in cores:
                chunk(source, target, k, r2, duo2, core2)

        far_chips(visit)

    def send_near(source, target, k):
        pltpu.make_async_copy(source.at[me], target.at[me], sem_recv.at[k]).start()
        chunk(source, target, k, r, duo, other)

    def arrived(array, k):
        pltpu.make_async_copy(array, array, sem_recv.at[k]).wait()

    def sent(array, k):
        pltpu.make_async_copy(array, array, sem_send.at[k]).wait()

    def make_edges(t, base, normed, mask):
        for a in range(OWN):
            x = normed[a]
            m = mask[a : a + 1, :]
            for side in range(2):
                g = dot(wt_in[t, pl.ds(2 * side * C + base, 32), :], x)
                v = dot(wt_in[t, pl.ds((2 * side + 1) * C + base, 32), :], x)
                e = jax.nn.sigmoid(g) * v * m
                for b in range(4):
                    wide[pl.ds(base * 32 + side * 16 + a * 4 + b, 32, stride=32), :] = e[
                        :, b * 128 : (b + 1) * 128
                    ]
        part = wide[pl.ds(pl.multiple_of(base * 32, 1024), 1024), :]
        send_a[t, pl.ds(base, 32)] = part.reshape(32, 32, 128).astype(BF16)

    for n in range(5):
        gain_b[n] = jnp.transpose(jnp.broadcast_to(gains[n : n + 1, :], (C, C)))
    for t in range(2):
        for g in range(5):
            part = w_in[t, :, g * C : (g + 1) * C].astype(F32)
            wt_in[t, g * C : (g + 1) * C, :] = jnp.transpose(part).astype(BF16)
        wt_out[t] = jnp.transpose(w_out[t].astype(F32)).astype(BF16)
    wt_k[...] = jnp.transpose(w_attn[:, C : 2 * C].astype(F32)).astype(BF16)

    block_of = lax.broadcasted_iota(jnp.int32, (1, N), 1) // 64
    linked = jnp.zeros((1, N), jnp.int32)
    for nb in range(8):
        linked = jnp.where(block_of == nb, block_s[r, nb], linked)
    for i in range(2 * OWN):
        at = place if i < OWN else other * 8 + duo
        own_chain = chain_s[r * 64 + (i % OWN) * 16 + at]
        allowed = jnp.logical_or(chain_v[...] == own_chain, linked == 1)
        keep8[i : i + 1, :] = jnp.where(allowed, 1.0, 0.0).astype(F32)

    lane = lax.broadcasted_iota(jnp.int32, (1, C), 1)
    row_of = lax.rem(lane, 64)

    def pick(il, chains):
        return jnp.where(row_of == il, chain_s[r * 64 + il], chains)

    row_chain = lax.fori_loop(0, 64, pick, jnp.zeros((1, C), jnp.int32))
    block_on = block_s[r, duo]
    for s in range(16):
        col_chain = jnp.where(lane < 64, chain_s[c * 32 + s], chain_s[c * 32 + 16 + s])
        allowed = jnp.logical_or(row_chain == col_chain, block_on == 1)
        keep_0[s // 4 : s // 4 + 1, (s % 4) * 128 : (s % 4 + 1) * 128] = jnp.where(
            allowed, 1.0, 0.0
        ).astype(F32)

    wide[0:2048, :] = pair[...].astype(F32).reshape(2048, C)

    @pl.loop(0, 4)
    def _(a):
        for b in range(4):
            s = a * 4 + b
            x = jnp.concatenate(
                [wide[pl.ds(s, 64, stride=32), :], wide[pl.ds(16 + s, 64, stride=32), :]], axis=0
            )
            norm_0[a, :, b * 128 : (b + 1) * 128] = norm_cm(jnp.transpose(x), gain_b[0]).astype(
                BF16
            )

    @pl.loop(0, 4)
    def _(step):
        make_edges(0, pl.multiple_of(step * 32, 32), norm_0, keep_0)

    pl.semaphore_wait(barrier, DEV - 1)

    send_far(send_a.at[0], recv_a.at[0], 1, (0, 1))
    send_near(send_a.at[0], recv_a.at[0], 1)

    pltpu.make_async_copy(
        pair.at[:, place], rows_in.at[:, pl.ds(c * 32, 32)], sem_recv.at[0]
    ).start()

    @pl.loop(1, COLS)
    def _(step):
        t = lax.rem(c + step, COLS)
        pltpu.make_async_remote_copy(
            pair.at[:, lax.rem(t, 2) * 8 + lax.div(t, 2)],
            rows_in.at[:, pl.ds(c * 32, 32)],
            sem_send.at[0],
            sem_recv.at[0],
            device_id=(r, t),
            device_id_type=MESH,
        ).start()

    def triangle(t, k):
        arrived(recv_a.at[t], k)
        if t == 0:
            low = lax.broadcasted_iota(jnp.int32, (C, C), 1) < 64
            for side in range(2):
                for q in range(4):

                    @pl.loop(0, 2)
                    def _(k2):
                        first = k2 * CHIPS + 2 * q * 8
                        here = recv_a[t, pl.ds(first, 8), side * 16 : side * 16 + 16]
                        there = recv_a[t, pl.ds(first + 8, 8), side * 16 : side * 16 + 16]
                        here = here.astype(F32).reshape(C, C)
                        there = there.astype(F32).reshape(C, C)
                        at = pl.multiple_of(k2 * 128, 128)
                        edges[side, pl.ds(at, 128), q * 128 : (q + 1) * 128] = jnp.where(
                            low, here, pltpu.roll(there, 64, 1)
                        ).astype(BF16)
                        edges[side, pl.ds(at + 256, 128), q * 128 : (q + 1) * 128] = jnp.where(
                            low, pltpu.roll(here, 64, 1), there
                        ).astype(BF16)
        else:
            wide[...] = recv_a[t].astype(F32).reshape(4096, 128)
            for side in range(2):
                for b in range(4):

                    @pl.loop(0, OWN)
                    def _(a):
                        block = wide[pl.ds(side * 16 + a * 4 + b, 128, stride=32), :]
                        edges[
                            side, pl.ds(pl.multiple_of(a * 128, 128), 128), b * 128 : (b + 1) * 128
                        ] = block.astype(BF16)

        @pl.loop(0, 4)
        def _(q):
            left = edges[0, :, pl.ds(pl.multiple_of(q * 128, 128), 128)]
            total = dot(jnp.transpose(left.astype(F32)).astype(BF16), edges[1])
            for half in range(2):
                for a in range(OWN):
                    for k2 in range(2):
                        for b in range(4):
                            at = (k2 * CHIPS + (2 * q + half) * 8) * 16 + a * 4 + b
                            row = half * 64 + a * 16 + k2 * 8
                            wide[pl.ds(at, 8, stride=16), :] = total[
                                row : row + 8, b * 128 : (b + 1) * 128
                            ]

        send_b[t] = wide[0:2048, :].reshape(128, 16, 128).astype(BF16)
        send_far(send_b.at[t], recv_b.at[t], k + 1, (0, 1))
        send_near(send_b.at[t], recv_b.at[t], k + 1)

    def gates(t):
        for a in range(OWN):
            gate_cm[a] = jax.nn.sigmoid(dot(wt_in[t, 4 * C : 5 * C, :], norm8[a]))

    def finish(t, k, then):
        arrived(recv_b.at[t], k)
        wide[0:2048, :] = recv_b[t].astype(F32).reshape(2048, 128)

        @pl.loop(0, OWN)
        def _(a):
            total = jnp.concatenate(
                [wide[pl.ds(a * 4 + b, 128, stride=16), :] for b in range(4)], axis=1
            )
            normed = norm_cm(total, jnp.tile(gain_b[2 * t + 1], (1, 4))).astype(BF16)
            update = gate_cm[a] * dot(wt_out[t], normed)
            new = (pair_cm[a] + update).astype(BF16).astype(F32)
            pair_cm[a] = new
            then(a, norm_cm(new, jnp.tile(gain_b[2 * t + 2], (1, 4))).astype(BF16))

    triangle(0, 1)

    arrived(rows_in, 0)

    @pl.loop(0, OWN)
    def _(a):
        x = jnp.transpose(rows_in[a].astype(F32))
        pair_cm[a] = x
        norm8[a] = norm_cm(x, jnp.tile(gain_b[0], (1, 4))).astype(BF16)

    gates(0)

    def keep_norm(a, normed):
        norm8[a] = normed

    finish(0, 2, keep_norm)

    for half in range(2):

        @pl.loop(2 * half, 2 * half + 2)
        def _(step):
            make_edges(1, pl.multiple_of(step * 32, 32), norm8, keep8)

        send_far(send_a.at[1], recv_a.at[1], 3, (half,))
    send_near(send_a.at[1], recv_a.at[1], 3)
    gates(1)
    triangle(1, 3)

    sibling = (r, duo * 2 + other)
    own_half = pl.multiple_of(core * HALF, HALF)

    def bias_part(a, normed):
        norm8[a] = normed
        bias = dot(w_bias[...], normed)
        for h in range(H):
            for kb in range(4):
                wide[pl.ds(2048 + h * 16 + kb * 4 + a, 1), :] = bias[
                    h : h + 1, kb * 128 : (kb + 1) * 128
                ]
        half_send[a] = pair_cm[a, :, pl.ds(pl.multiple_of(other * HALF, HALF), HALF)].astype(BF16)
        resid8[a] = pair_cm[a, :, pl.ds(own_half, HALF)].astype(BF16)

    finish(1, 4, bias_part)
    bias_send[...] = wide[2048 : 2048 + 64, :].reshape(H, 16, 128).astype(BF16)

    asks = lax.div(r, 4)
    slot = cy * 16 + place
    for h in range(H):

        def visit(r2, duo2):
            pltpu.make_async_remote_copy(
                bias_send.at[h],
                bias_recv.at[h, slot],
                sem_send.at[5],
                sem_recv.at[5 + h],
                device_id=(r2, duo2 * 2 + asks),
                device_id_type=MESH,
            ).start()

        far_chips(visit)

        @pl.when(asks == core)
        def _():
            pltpu.make_async_copy(
                bias_send.at[h], bias_recv.at[h, slot], sem_recv.at[5 + h]
            ).start()

        @pl.when(asks != core)
        def _():
            pltpu.make_async_remote_copy(
                bias_send.at[h],
                bias_recv.at[h, slot],
                sem_send.at[5],
                sem_recv.at[5 + h],
                device_id=sibling,
                device_id_type=MESH,
            ).start()

        if h == 0:
            pltpu.make_async_remote_copy(
                norm8.at[pl.ds(0, OWN)],
                norm8.at[pl.ds(OWN, OWN)],
                sem_send.at[6],
                sem_recv.at[9],
                device_id=sibling,
                device_id_type=MESH,
            ).start()
            pltpu.make_async_remote_copy(
                half_send,
                resid8.at[pl.ds(OWN, OWN)],
                sem_send.at[7],
                sem_recv.at[10],
                device_id=sibling,
                device_id_type=MESH,
            ).start()

    lane_q = lax.broadcasted_iota(jnp.int32, (HALF, C), 1)
    lane_v = lax.broadcasted_iota(jnp.int32, (N, C), 1)
    first_lane = jnp.where(lane_q == 0, 1.0, 0.0).astype(BF16)
    first_row = lax.broadcasted_iota(jnp.int32, (C, N), 0) == 0

    def prepare(i):
        k_ext[i, 0:C, :] = dot(wt_k[...], norm8[i]).astype(BF16)
        penalty = jnp.where(keep8[pl.ds(i, 1), :] > 0.5, 0.0, -1e9)
        k_ext[i, C:, :] = jnp.where(first_row, penalty, 0.0).astype(BF16)
        rows_in[0] = jnp.transpose(norm8[i].astype(F32)).astype(BF16)
        values = dot(rows_in[0], w_attn[:, 2 * C : 3 * C])
        asked = rows_in[0, pl.ds(own_half, HALF), :]
        queries = dot(asked, w_attn[:, 0:C]) * (32**-0.5 * LOG2E)
        gate8[i] = jax.nn.sigmoid(dot(asked, w_attn[:, 3 * C :]))
        for h in range(H):
            here_q = jnp.logical_and(lane_q >= 32 * h, lane_q < 32 * (h + 1))
            here_v = jnp.logical_and(lane_v >= 32 * h, lane_v < 32 * (h + 1))
            q_ext[i, h, :, 0:C] = jnp.where(here_q, queries, 0.0).astype(BF16)
            q_ext[i, h, :, C:] = first_lane
            v_ext[i, h, :, 0:C] = jnp.where(here_v, values, 0.0).astype(BF16)
            v_ext[i, h, :, C:] = jnp.ones((N, C), BF16)

    pl.loop(0, OWN)(prepare)
    arrived(norm8.at[pl.ds(OWN, OWN)], 9)
    pl.loop(OWN, 2 * OWN)(prepare)
    arrived(resid8.at[pl.ds(OWN, OWN)], 10)

    for h in range(H):
        arrived(bias_recv.at[h], 5 + h)
        wide[0:1024, :] = bias_recv[h].astype(F32).reshape(1024, 128) * LOG2E
        for y in range(4):
            for a in range(OWN):
                for kb in range(4):
                    bias_nat[
                        y * 64 + a * 16 : y * 64 + a * 16 + 16, kb * 128 : (kb + 1) * 128
                    ] = wide[pl.ds(y * 256 + kb * 4 + a, 16, stride=16), :]

        @pl.loop(0, 2 * OWN)
        def _(i):
            scores = dot(q_ext[i, h], k_ext[i]) + bias_nat[...]
            mixed = dot(jnp.exp2(scores).astype(BF16), v_ext[i, h])
            part = mixed[:, 0:C] / mixed[:, C:]
            if h == 0:
                total8[i] = part
            elif h < H - 1:
                total8[i] += part
            else:
                gated = (gate8[i] * (total8[i] + part)).astype(BF16)
                update = dot(gated, w_final[...])
                rows_out[i] = (jnp.transpose(resid8[i].astype(F32)) + update).astype(BF16)
                a = lax.rem(i, OWN)
                owner = lax.rem(core + lax.div(i, OWN), 2) * 8 + duo

                @pl.loop(0, 8)
                def _(u):
                    source = rows_out.at[i, pl.ds(u * 32, 32)]
                    target = out.at[a, owner]

                    @pl.when(core * 8 + u == c)
                    def _():
                        pltpu.make_async_copy(source, target, sem_recv.at[11]).start()

                    @pl.when(core * 8 + u != c)
                    def _():
                        pltpu.make_async_remote_copy(
                            source,
                            target,
                            sem_send.at[8],
                            sem_recv.at[11],
                            device_id=(r, core * 8 + u),
                            device_id_type=MESH,
                        ).start()

    arrived(out, 11)

    sent(out.at[:, pl.ds(0, COLS - 1)], 0)
    for t in range(2):
        sent(recv_a.at[t, pl.ds(0, DEV - 1)], 2 * t + 1)
        sent(recv_b.at[t, pl.ds(0, DEV - 1)], 2 * t + 2)
    sent(norm8.at[pl.ds(0, OWN)], 6)
    sent(half_send, 7)

    @pl.when(asks == core)
    def _():
        sent(bias_recv.at[:, pl.ds(0, CHIPS - 1)], 5)

    @pl.when(asks != core)
    def _():
        sent(bias_recv, 5)

    @pl.when(lax.div(c, 8) == core)
    def _():
        sent(out.at[:, pl.ds(0, COLS - 2)], 8)

    @pl.when(lax.div(c, 8) != core)
    def _():
        sent(out, 8)


def per_device(
    pair, chain_id, block_mask, norm_gains, w_in, w_out, w_attn, w_bias, w_final
):
    vmem = pl.BlockSpec(memory_space=pltpu.VMEM)
    smem = pl.BlockSpec(memory_space=pltpu.SMEM)
    result = pl.pallas_call(
        kernel,
        out_shape=jax.ShapeDtypeStruct((OWN, COLS, 32, C), BF16),
        in_specs=[vmem, smem, vmem, smem] + [vmem] * 6,
        out_specs=vmem,
        scratch_shapes=[
            pltpu.VMEM((OWN, N, C), BF16),
            pltpu.VMEM((OWN, C, N), F32),
            pltpu.VMEM((OWN, C, N), F32),
            pltpu.VMEM((2 * OWN, C, N), BF16),
            pltpu.VMEM((OWN, C, N), BF16),
            pltpu.VMEM((2 * OWN, N), F32),
            pltpu.VMEM((8, N), F32),
            pltpu.VMEM((5, C, C), F32),
            pltpu.VMEM((2, 5 * C, C), BF16),
            pltpu.VMEM((2, C, C), BF16),
            pltpu.VMEM((C, C), BF16),
            pltpu.VMEM((4096, C), F32),
            pltpu.VMEM((2, N, N), BF16),
            pltpu.VMEM((2, DEV, 32, C), BF16),
            pltpu.VMEM((2, DEV, 32, C), BF16),
            pltpu.VMEM((2, DEV, 16, C), BF16),
            pltpu.VMEM((2, DEV, 16, C), BF16),
            pltpu.VMEM((H, 16, C), BF16),
            pltpu.VMEM((H, CHIPS, 16, C), BF16),
            pltpu.VMEM((HALF, N), F32),
            pltpu.VMEM((OWN, C, HALF), BF16),
            pltpu.VMEM((2 * OWN, C, HALF), BF16),
            pltpu.VMEM((2 * OWN, H, HALF, 2 * C), BF16),
            pltpu.VMEM((2 * OWN, 2 * C, N), BF16),
            pltpu.VMEM((2 * OWN, H, N, 2 * C), BF16),
            pltpu.VMEM((2 * OWN, HALF, C), F32),
            pltpu.VMEM((2 * OWN, HALF, C), F32),
            pltpu.VMEM((2 * OWN, HALF, C), BF16),
            pltpu.SemaphoreType.DMA((9,)),
            pltpu.SemaphoreType.DMA((12,)),
        ],
        name="triangle_block",
        compiler_params=pltpu.CompilerParams(
            collective_id=0, has_side_effects=True, vmem_limit_bytes=60 << 20
        ),
        cost_estimate=pl.CostEstimate(
            flops=3 * 10**9, bytes_accessed=2 * 10**6, transcendentals=5 * 10**6
        ),
    )(
        pair.reshape(OWN, COLS, 32, C),
        chain_id,
        chain_id.reshape(1, N),
        block_mask,
        norm_gains,
        w_in,
        w_out,
        w_attn,
        w_bias.T,
        w_final,
    )
    return result.reshape(64, 32, C)


def solution(mesh):
    placed = (P("row", "col", None), P(), P(), P(), P(), P(), P(), P(), P())
    return jax.shard_map(
        per_device, mesh=mesh, in_specs=placed, out_specs=P("row", "col", None), check_vma=False
    )
```

```python
import jax
import jax.numpy as jnp
from jax import lax
from jax.experimental import pallas as pl
from jax.experimental.pallas import tpu as pltpu
from jax.sharding import PartitionSpec as P

MESH = pl.DeviceIdType.MESH
F32 = jnp.float32
BF16 = jnp.bfloat16
ROWS = 8
COLS = 16
DEV = ROWS * COLS
CHIPS = DEV // 2
C = 128
N = 512
HALF = N // 2
H = 4
OWN = 4
LOG2E = 1.4426950408889634

FAR = (
    (699248298, 5),
    (791255470, 5),
    (966748069, 5),
    (770581915, 5),
    (199256638, 5),
    (744454258, 5),
    (160421045, 5),
    (612196317, 5),
    (322204568, 5),
    (336278469, 5),
    (539184252, 5),
    (51578641, 5),
    (49232, 3),
)


def dot(a, b):
    return jnp.dot(a, b, preferred_element_type=F32)


def inverse(x):
    guess = pltpu.reciprocal(x, approx=True)
    return guess * (2.0 - x * guess)


def norm_cm(x, gain):
    center = x - jnp.mean(x, axis=0, keepdims=True)
    spread = jnp.mean(center * center, axis=0, keepdims=True)
    return center * lax.rsqrt(spread + 1e-05) * gain


def kernel(
    pair,
    chain_s,
    chain_v,
    block_s,
    gains,
    w_in,
    w_out,
    w_attn,
    w_bias,
    w_final,
    out,
    rows_in,
    pair_cm,
    gate_cm,
    norm8,
    norm_0,
    keep8,
    keep_0,
    gain_b,
    wt_in,
    wt_out,
    wt_k,
    wide,
    edges,
    send_a,
    recv_a,
    send_b,
    recv_b,
    bias_send,
    bias_recv,
    bias_nat,
    half_send,
    resid8,
    q_ext,
    k_ext,
    v_ext,
    gate8,
    total8,
    rows_out,
    sem_send,
    sem_recv,
):
    r = lax.axis_index("row")
    c = lax.axis_index("col")
    core = lax.rem(c, 2)
    duo = lax.div(c, 2)
    chip = r * 8 + duo
    me = core * CHIPS + chip
    place = core * 8 + duo
    other = 1 - core
    cx = lax.rem(duo, 2) * 2 + lax.div(r, 4)
    cy = lax.rem(r, 4)
    cz = lax.div(duo, 2)

    barrier = pltpu.get_barrier_semaphore()

    @pl.loop(1, DEV)
    def _(step):
        t = lax.rem(r * COLS + c + step, DEV)
        pl.semaphore_signal(
            barrier, inc=1, device_id=(lax.div(t, COLS), lax.rem(t, COLS)), device_id_type=MESH
        )

    def far_chips(visit):
        for packed, count in FAR:

            def body(_, value):
                d = lax.rem(value, 64)
                x = lax.rem(cx + lax.rem(d, 4), 4)
                y = lax.rem(cy + lax.rem(lax.div(d, 4), 4), 4)
                z = lax.rem(cz + lax.div(d, 16), 4)
                visit(lax.rem(x, 2) * 4 + y, z * 2 + lax.div(x, 2))
                return lax.div(value, 64)

            lax.fori_loop(0, count, body, jnp.int32(packed))

    def chunk(source, target, k, r2, duo2, core2):
        t = core2 * CHIPS + r2 * 8 + duo2
        pltpu.make_async_remote_copy(
            source.at[t],
            target.at[me],
            sem_send.at[k],
            sem_recv.at[k],
            device_id=(r2, duo2 * 2 + core2),
            device_id_type=MESH,
        ).start()

    def send_far(source, target, k, cores):
        def visit(r2, duo2):
            for core2 in cores:
                chunk(source, target, k, r2, duo2, core2)

        far_chips(visit)

    def send_near(source, target, k):
        pltpu.make_async_copy(source.at[me], target.at[me], sem_recv.at[k]).start()
        chunk(source, target, k, r, duo, other)

    def arrived(array, k):
        pltpu.make_async_copy(array, array, sem_recv.at[k]).wait()

    def sent(array, k):
        pltpu.make_async_copy(array, array, sem_send.at[k]).wait()

    def make_edges(t, base, normed, mask):
        for a in range(OWN):
            x = normed[a]
            m = mask[a : a + 1, :]
            for side in range(2):
                g = dot(wt_in[t, pl.ds(2 * side * C + base, 32), :], x)
                v = dot(wt_in[t, pl.ds((2 * side + 1) * C + base, 32), :], x)
                e = jax.nn.sigmoid(g) * v * m
                for b in range(4):
                    wide[pl.ds(base * 32 + side * 16 + a * 4 + b, 32, stride=32), :] = e[
                        :, b * 128 : (b + 1) * 128
                    ]
        part = wide[base * 32 : base * 32 + 1024, :]
        send_a[t, base : base + 32] = part.reshape(32, 32, 128).astype(BF16)

    def set_in(t):
        for g in range(5):
            part = w_in[t, :, g * C : (g + 1) * C].astype(F32)
            wt_in[t, g * C : (g + 1) * C, :] = jnp.transpose(part).astype(BF16)

    def set_gain(n):
        gain_b[n] = jnp.transpose(jnp.broadcast_to(gains[n : n + 1, :], (C, C)))

    set_in(0)
    set_gain(0)

    lane = lax.broadcasted_iota(jnp.int32, (1, C), 1)
    row_of = lax.rem(lane, 64)

    def pick(il, chains):
        return jnp.where(row_of == il, chain_s[r * 64 + il], chains)

    row_chain = lax.fori_loop(0, 64, pick, jnp.zeros((1, C), jnp.int32))
    block_on = block_s[r, duo]
    for s in range(16):
        col_chain = jnp.where(lane < 64, chain_s[c * 32 + s], chain_s[c * 32 + 16 + s])
        allowed = jnp.logical_or(row_chain == col_chain, block_on == 1)
        keep_0[s // 4 : s // 4 + 1, (s % 4) * 128 : (s % 4 + 1) * 128] = jnp.where(
            allowed, 1.0, 0.0
        ).astype(F32)

    wide[0:2048, :] = pair[...].astype(F32).reshape(2048, C)

    for a in range(4):
        for b in range(4):
            s = a * 4 + b
            x = jnp.concatenate(
                [wide[pl.ds(s, 64, stride=32), :], wide[pl.ds(16 + s, 64, stride=32), :]], axis=0
            )
            norm_0[a, :, b * 128 : (b + 1) * 128] = norm_cm(jnp.transpose(x), gain_b[0]).astype(
                BF16
            )

    for half in range(2):
        for step in (2 * half, 2 * half + 1):
            make_edges(0, step * 32, norm_0, keep_0)
        if half == 0:
            pl.semaphore_wait(barrier, DEV - 1)
        send_far(send_a.at[0], recv_a.at[0], 1, (half,))
    send_near(send_a.at[0], recv_a.at[0], 1)

    pltpu.make_async_copy(
        pair.at[:, place], rows_in.at[:, pl.ds(c * 32, 32)], sem_recv.at[0]
    ).start()

    @pl.loop(1, COLS)
    def _(step):
        t = lax.rem(c + step, COLS)
        pltpu.make_async_remote_copy(
            pair.at[:, lax.rem(t, 2) * 8 + lax.div(t, 2)],
            rows_in.at[:, pl.ds(c * 32, 32)],
            sem_send.at[0],
            sem_recv.at[0],
            device_id=(r, t),
            device_id_type=MESH,
        ).start()

    for n in range(1, 5):
        set_gain(n)
    set_in(1)
    for t in range(2):
        wt_out[t] = jnp.transpose(w_out[t].astype(F32)).astype(BF16)
    wt_k[...] = jnp.transpose(w_attn[:, C : 2 * C].astype(F32)).astype(BF16)

    block_of = lax.broadcasted_iota(jnp.int32, (1, N), 1) // 64
    linked = jnp.zeros((1, N), jnp.int32)
    for nb in range(8):
        linked = jnp.where(block_of == nb, block_s[r, nb], linked)
    for i in range(2 * OWN):
        at = place if i < OWN else other * 8 + duo
        own_chain = chain_s[r * 64 + (i % OWN) * 16 + at]
        allowed = jnp.logical_or(chain_v[...] == own_chain, linked == 1)
        keep8[i : i + 1, :] = jnp.where(allowed, 1.0, 0.0).astype(F32)

    def triangle(t, k):
        arrived(recv_a.at[t], k)
        if t == 0:
            low = lax.broadcasted_iota(jnp.int32, (C, C), 1) < 64
            for side in range(2):
                for q in range(4):
                    for k2 in range(2):
                        first = k2 * CHIPS + 2 * q * 8
                        here = recv_a[t, pl.ds(first, 8), side * 16 : side * 16 + 16]
                        there = recv_a[t, pl.ds(first + 8, 8), side * 16 : side * 16 + 16]
                        here = here.astype(F32).reshape(C, C)
                        there = there.astype(F32).reshape(C, C)
                        at = k2 * 128
                        edges[side, pl.ds(at, 128), q * 128 : (q + 1) * 128] = jnp.where(
                            low, here, pltpu.roll(there, 64, 1)
                        ).astype(BF16)
                        edges[side, pl.ds(at + 256, 128), q * 128 : (q + 1) * 128] = jnp.where(
                            low, pltpu.roll(here, 64, 1), there
                        ).astype(BF16)
        else:
            wide[...] = recv_a[t].astype(F32).reshape(4096, 128)
            for side in range(2):
                for b in range(4):
                    for a in range(OWN):
                        block = wide[pl.ds(side * 16 + a * 4 + b, 128, stride=32), :]
                        edges[
                            side, a * 128 : (a + 1) * 128, b * 128 : (b + 1) * 128
                        ] = block.astype(BF16)

        for q in range(4):
            left = edges[0, :, q * 128 : (q + 1) * 128]
            total = dot(jnp.transpose(left.astype(F32)).astype(BF16), edges[1])
            for half in range(2):
                for a in range(OWN):
                    for k2 in range(2):
                        for b in range(4):
                            at = (k2 * CHIPS + (2 * q + half) * 8) * 16 + a * 4 + b
                            row = half * 64 + a * 16 + k2 * 8
                            wide[pl.ds(at, 8, stride=16), :] = total[
                                row : row + 8, b * 128 : (b + 1) * 128
                            ]

        send_b[t] = wide[0:2048, :].reshape(128, 16, 128).astype(BF16)
        send_far(send_b.at[t], recv_b.at[t], k + 1, (0, 1))
        send_near(send_b.at[t], recv_b.at[t], k + 1)

    def gates(t):
        for a in range(OWN):
            gate_cm[a] = jax.nn.sigmoid(dot(wt_in[t, 4 * C : 5 * C, :], norm8[a]))

    def finish(t, k, then):
        arrived(recv_b.at[t], k)
        wide[0:2048, :] = recv_b[t].astype(F32).reshape(2048, 128)

        for a in range(OWN):
            total = jnp.concatenate(
                [wide[pl.ds(a * 4 + b, 128, stride=16), :] for b in range(4)], axis=1
            )
            normed = norm_cm(total, jnp.tile(gain_b[2 * t + 1], (1, 4))).astype(BF16)
            update = gate_cm[a] * dot(wt_out[t], normed)
            new = (pair_cm[a] + update).astype(BF16).astype(F32)
            pair_cm[a] = new
            then(a, norm_cm(new, jnp.tile(gain_b[2 * t + 2], (1, 4))).astype(BF16))

    triangle(0, 1)

    arrived(rows_in, 0)
    for a in range(OWN):
        x = jnp.transpose(rows_in[a].astype(F32))
        pair_cm[a] = x
        norm8[a] = norm_cm(x, jnp.tile(gain_b[0], (1, 4))).astype(BF16)

    gates(0)

    def keep_norm(a, normed):
        norm8[a] = normed

    finish(0, 2, keep_norm)

    for half in range(2):
        for step in (2 * half, 2 * half + 1):
            make_edges(1, step * 32, norm8, keep8)

        send_far(send_a.at[1], recv_a.at[1], 3, (half,))
    send_near(send_a.at[1], recv_a.at[1], 3)
    gates(1)
    triangle(1, 3)

    sibling = (r, duo * 2 + other)
    own_half = pl.multiple_of(core * HALF, HALF)

    def bias_part(a, normed):
        norm8[a] = normed
        bias = dot(w_bias[...], normed)
        for h in range(H):
            for kb in range(4):
                wide[pl.ds(2048 + h * 16 + kb * 4 + a, 1), :] = bias[
                    h : h + 1, kb * 128 : (kb + 1) * 128
                ]
        half_send[a] = pair_cm[a, :, pl.ds(pl.multiple_of(other * HALF, HALF), HALF)].astype(BF16)
        resid8[a] = pair_cm[a, :, pl.ds(own_half, HALF)].astype(BF16)

    finish(1, 4, bias_part)
    bias_send[...] = wide[2048 : 2048 + 64, :].reshape(H, 16, 128).astype(BF16)

    asks = lax.div(r, 4)
    slot = cy * 16 + place
    for h in range(H):

        def visit(r2, duo2):
            pltpu.make_async_remote_copy(
                bias_send.at[h],
                bias_recv.at[h, slot],
                sem_send.at[5],
                sem_recv.at[5 + h],
                device_id=(r2, duo2 * 2 + asks),
                device_id_type=MESH,
            ).start()

        far_chips(visit)

        @pl.when(asks == core)
        def _():
            pltpu.make_async_copy(
                bias_send.at[h], bias_recv.at[h, slot], sem_recv.at[5 + h]
            ).start()

        @pl.when(asks != core)
        def _():
            pltpu.make_async_remote_copy(
                bias_send.at[h],
                bias_recv.at[h, slot],
                sem_send.at[5],
                sem_recv.at[5 + h],
                device_id=sibling,
                device_id_type=MESH,
            ).start()

        if h == 0:
            pltpu.make_async_remote_copy(
                norm8.at[pl.ds(0, OWN)],
                norm8.at[pl.ds(OWN, OWN)],
                sem_send.at[6],
                sem_recv.at[9],
                device_id=sibling,
                device_id_type=MESH,
            ).start()
            pltpu.make_async_remote_copy(
                half_send,
                resid8.at[pl.ds(OWN, OWN)],
                sem_send.at[7],
                sem_recv.at[10],
                device_id=sibling,
                device_id_type=MESH,
            ).start()

    lane_q = lax.broadcasted_iota(jnp.int32, (HALF, C), 1)
    lane_v = lax.broadcasted_iota(jnp.int32, (N, C), 1)
    first_lane = jnp.where(lane_q == 0, 1.0, 0.0).astype(BF16)
    first_row = lax.broadcasted_iota(jnp.int32, (C, N), 0) == 0

    def prepare(i):
        k_ext[i, 0:C, :] = dot(wt_k[...], norm8[i]).astype(BF16)
        penalty = jnp.where(keep8[pl.ds(i, 1), :] > 0.5, 0.0, -1e9)
        k_ext[i, C:, :] = jnp.where(first_row, penalty, 0.0).astype(BF16)
        rows_in[0] = jnp.transpose(norm8[i].astype(F32)).astype(BF16)
        values = dot(rows_in[0], w_attn[:, 2 * C : 3 * C])
        asked = rows_in[0, pl.ds(own_half, HALF), :]
        queries = dot(asked, w_attn[:, 0:C]) * (32**-0.5 * LOG2E)
        gate8[i] = jax.nn.sigmoid(dot(asked, w_attn[:, 3 * C :]))
        for h in range(H):
            here_q = jnp.logical_and(lane_q >= 32 * h, lane_q < 32 * (h + 1))
            here_v = jnp.logical_and(lane_v >= 32 * h, lane_v < 32 * (h + 1))
            q_ext[i, h, :, 0:C] = jnp.where(here_q, queries, 0.0).astype(BF16)
            q_ext[i, h, :, C:] = first_lane
            v_ext[i, h, :, 0:C] = jnp.where(here_v, values, 0.0).astype(BF16)
            v_ext[i, h, :, C:] = jnp.ones((N, C), BF16)

    pl.loop(0, OWN)(prepare)
    arrived(norm8.at[pl.ds(OWN, OWN)], 9)
    pl.loop(OWN, 2 * OWN)(prepare)
    arrived(resid8.at[pl.ds(OWN, OWN)], 10)

    def out_part(i, u):
        owner = (core if i < OWN else other) * 8 + duo
        return rows_out.at[i, pl.ds(pl.multiple_of(u * 32, 32), 32)], out.at[i % OWN, owner]

    def send_out(i, u):
        source, target = out_part(i, u)
        pltpu.make_async_remote_copy(
            source,
            target,
            sem_send.at[8],
            sem_recv.at[11],
            device_id=(r, core * 8 + u),
            device_id_type=MESH,
        ).start()

    for h in range(H):
        arrived(bias_recv.at[h], 5 + h)
        wide[0:1024, :] = bias_recv[h].astype(F32).reshape(1024, 128) * LOG2E
        for y in range(4):
            for a in range(OWN):
                for kb in range(4):
                    bias_nat[
                        y * 64 + a * 16 : y * 64 + a * 16 + 16, kb * 128 : (kb + 1) * 128
                    ] = wide[pl.ds(y * 256 + kb * 4 + a, 16, stride=16), :]

        for i in range(2 * OWN):
            scores = dot(q_ext[i, h], k_ext[i]) + bias_nat[...]
            mixed = dot(jnp.exp2(scores).astype(BF16), v_ext[i, h])
            part = mixed[:, 0:C] * inverse(mixed[:, C:])
            if h == 0:
                total8[i] = part
            elif h < H - 1:
                total8[i] += part
            else:
                gated = (gate8[i] * (total8[i] + part)).astype(BF16)
                update = dot(gated, w_final[...])
                rows_out[i] = (jnp.transpose(resid8[i].astype(F32)) + update).astype(BF16)
                for u in range(1, 8):
                    send_out(i, lax.rem(c + u, 8))

    @pl.when(lax.div(c, 8) == core)
    def _():
        for i in range(2 * OWN):
            source, target = out_part(i, lax.rem(c, 8))
            pltpu.make_async_copy(source, target, sem_recv.at[11]).start()

    @pl.when(lax.div(c, 8) != core)
    def _():
        for i in range(2 * OWN):
            send_out(i, lax.rem(c, 8))

    arrived(out, 11)

    sent(out.at[:, pl.ds(0, COLS - 1)], 0)
    for t in range(2):
        sent(recv_a.at[t, pl.ds(0, DEV - 1)], 2 * t + 1)
        sent(recv_b.at[t, pl.ds(0, DEV - 1)], 2 * t + 2)
    sent(norm8.at[pl.ds(0, OWN)], 6)
    sent(half_send, 7)

    @pl.when(asks == core)
    def _():
        sent(bias_recv.at[:, pl.ds(0, CHIPS - 1)], 5)

    @pl.when(asks != core)
    def _():
        sent(bias_recv, 5)

    @pl.when(lax.div(c, 8) == core)
    def _():
        sent(out.at[:, pl.ds(0, COLS - 2)], 8)

    @pl.when(lax.div(c, 8) != core)
    def _():
        sent(out, 8)


def per_device(
    pair, chain_id, block_mask, norm_gains, w_in, w_out, w_attn, w_bias, w_final
):
    vmem = pl.BlockSpec(memory_space=pltpu.VMEM)
    smem = pl.BlockSpec(memory_space=pltpu.SMEM)
    result = pl.pallas_call(
        kernel,
        out_shape=jax.ShapeDtypeStruct((OWN, COLS, 32, C), BF16),
        in_specs=[vmem, smem, vmem, smem] + [vmem] * 6,
        out_specs=vmem,
        scratch_shapes=[
            pltpu.VMEM((OWN, N, C), BF16),
            pltpu.VMEM((OWN, C, N), F32),
            pltpu.VMEM((OWN, C, N), F32),
            pltpu.VMEM((2 * OWN, C, N), BF16),
            pltpu.VMEM((OWN, C, N), BF16),
            pltpu.VMEM((2 * OWN, N), F32),
            pltpu.VMEM((8, N), F32),
            pltpu.VMEM((5, C, C), F32),
            pltpu.VMEM((2, 5 * C, C), BF16),
            pltpu.VMEM((2, C, C), BF16),
            pltpu.VMEM((C, C), BF16),
            pltpu.VMEM((4096, C), F32),
            pltpu.VMEM((2, N, N), BF16),
            pltpu.VMEM((2, DEV, 32, C), BF16),
            pltpu.VMEM((2, DEV, 32, C), BF16),
            pltpu.VMEM((2, DEV, 16, C), BF16),
            pltpu.VMEM((2, DEV, 16, C), BF16),
            pltpu.VMEM((H, 16, C), BF16),
            pltpu.VMEM((H, CHIPS, 16, C), BF16),
            pltpu.VMEM((HALF, N), F32),
            pltpu.VMEM((OWN, C, HALF), BF16),
            pltpu.VMEM((2 * OWN, C, HALF), BF16),
            pltpu.VMEM((2 * OWN, H, HALF, 2 * C), BF16),
            pltpu.VMEM((2 * OWN, 2 * C, N), BF16),
            pltpu.VMEM((2 * OWN, H, N, 2 * C), BF16),
            pltpu.VMEM((2 * OWN, HALF, C), F32),
            pltpu.VMEM((2 * OWN, HALF, C), F32),
            pltpu.VMEM((2 * OWN, HALF, C), BF16),
            pltpu.SemaphoreType.DMA((9,)),
            pltpu.SemaphoreType.DMA((12,)),
        ],
        name="triangle_block",
        compiler_params=pltpu.CompilerParams(
            collective_id=0, has_side_effects=True, vmem_limit_bytes=60 << 20
        ),
        cost_estimate=pl.CostEstimate(
            flops=3 * 10**9, bytes_accessed=2 * 10**6, transcendentals=5 * 10**6
        ),
    )(
        pair.reshape(OWN, COLS, 32, C),
        chain_id,
        chain_id.reshape(1, N),
        block_mask,
        norm_gains,
        w_in,
        w_out,
        w_attn,
        w_bias.T,
        w_final,
    )
    return result.reshape(64, 32, C)


def solution(mesh):
    placed = (P("row", "col", None), P(), P(), P(), P(), P(), P(), P(), P())
    return jax.shard_map(
        per_device, mesh=mesh, in_specs=placed, out_specs=P("row", "col", None), check_vma=False
    )
```

```python
import jax
import jax.numpy as jnp
from jax import lax
from jax.experimental import pallas as pl
from jax.experimental.pallas import tpu as pltpu
from jax.sharding import PartitionSpec as P

MESH = pl.DeviceIdType.MESH
F32 = jnp.float32
BF16 = jnp.bfloat16
ROWS = 8
COLS = 16
DEV = ROWS * COLS
CHIPS = DEV // 2
C = 128
N = 512
HALF = N // 2
H = 4
OWN = 4
LOG2E = 1.4426950408889634

FAR = (
    (699248298, 5),
    (791255470, 5),
    (966748069, 5),
    (770581915, 5),
    (199256638, 5),
    (744454258, 5),
    (160421045, 5),
    (612196317, 5),
    (322204568, 5),
    (336278469, 5),
    (539184252, 5),
    (51578641, 5),
    (49232, 3),
)


def dot(a, b):
    return jnp.dot(a, b, preferred_element_type=F32)


def inverse(x):
    guess = pltpu.reciprocal(x, approx=True)
    return guess * (2.0 - x * guess)


def norm_cm(x, gain):
    center = x - jnp.mean(x, axis=0, keepdims=True)
    spread = jnp.mean(center * center, axis=0, keepdims=True)
    return center * lax.rsqrt(spread + 1e-05) * gain


def kernel(
    pair,
    chain_s,
    chain_v,
    block_s,
    gains,
    w_in,
    w_out,
    w_attn,
    w_bias,
    w_final,
    out,
    rows_in,
    pair_cm,
    gate_cm,
    norm8,
    norm_0,
    keep8,
    keep_0,
    gain_b,
    wt_in,
    wt_out,
    wt_k,
    wide,
    edges,
    send_a,
    recv_a,
    send_b,
    recv_b,
    bias_send,
    bias_recv,
    bias_nat,
    half_send,
    resid8,
    q_ext,
    k_ext,
    v_ext,
    gate8,
    total8,
    rows_out,
    sem_send,
    sem_recv,
):
    r = lax.axis_index("row")
    c = lax.axis_index("col")
    core = lax.rem(c, 2)
    duo = lax.div(c, 2)
    chip = r * 8 + duo
    me = core * CHIPS + chip
    place = core * 8 + duo
    other = 1 - core
    cx = lax.rem(duo, 2) * 2 + lax.div(r, 4)
    cy = lax.rem(r, 4)
    cz = lax.div(duo, 2)

    barrier = pltpu.get_barrier_semaphore()

    def greet(i, j):
        pl.semaphore_signal(
            barrier,
            inc=1,
            device_id=(lax.rem(r + i, ROWS), lax.rem(c + j, COLS)),
            device_id_type=MESH,
        )

    for j in range(1, COLS):
        greet(0, j)

    @pl.loop(1, ROWS)
    def _(i):
        for j in range(COLS):
            greet(i, j)

    def far_chips(visit):
        for packed, count in FAR:

            def body(_, value):
                d = lax.rem(value, 64)
                x = lax.rem(cx + lax.rem(d, 4), 4)
                y = lax.rem(cy + lax.rem(lax.div(d, 4), 4), 4)
                z = lax.rem(cz + lax.div(d, 16), 4)
                visit(lax.rem(x, 2) * 4 + y, z * 2 + lax.div(x, 2))
                return lax.div(value, 64)

            lax.fori_loop(0, count, body, jnp.int32(packed))

    def chunk(source, target, k, r2, duo2, core2):
        t = core2 * CHIPS + r2 * 8 + duo2
        pltpu.make_async_remote_copy(
            source.at[t],
            target.at[me],
            sem_send.at[k],
            sem_recv.at[k],
            device_id=(r2, duo2 * 2 + core2),
            device_id_type=MESH,
        ).start()

    def send_far(source, target, k, cores):
        def visit(r2, duo2):
            for core2 in cores:
                chunk(source, target, k, r2, duo2, core2)

        far_chips(visit)

    def send_near(source, target, k):
        pltpu.make_async_copy(source.at[me], target.at[me], sem_recv.at[k]).start()
        chunk(source, target, k, r, duo, other)

    def arrived(array, k):
        pltpu.make_async_copy(array, array, sem_recv.at[k]).wait()

    def sent(array, k):
        pltpu.make_async_copy(array, array, sem_send.at[k]).wait()

    def make_edges(t, base, normed, mask):
        for a in range(OWN):
            x = normed[a]
            m = mask[a : a + 1, :]
            for side in range(2):
                g = dot(wt_in[t, pl.ds(2 * side * C + base, 32), :], x)
                v = dot(wt_in[t, pl.ds((2 * side + 1) * C + base, 32), :], x)
                e = jax.nn.sigmoid(g) * v * m
                for b in range(4):
                    wide[pl.ds(base * 32 + side * 16 + a * 4 + b, 32, stride=32), :] = e[
                        :, b * 128 : (b + 1) * 128
                    ]
        part = wide[base * 32 : base * 32 + 1024, :]
        send_a[t, base : base + 32] = part.reshape(32, 32, 128).astype(BF16)

    def set_in(t):
        for g in range(5):
            part = w_in[t, :, g * C : (g + 1) * C].astype(F32)
            wt_in[t, g * C : (g + 1) * C, :] = jnp.transpose(part).astype(BF16)

    def set_gain(n):
        gain_b[n] = jnp.transpose(jnp.broadcast_to(gains[n : n + 1, :], (C, C)))

    set_in(0)
    set_gain(0)

    lane = lax.broadcasted_iota(jnp.int32, (1, C), 1)
    row_of = lax.rem(lane, 64)

    def pick(il, chains):
        return jnp.where(row_of == il, chain_s[r * 64 + il], chains)

    row_chain = lax.fori_loop(0, 64, pick, jnp.zeros((1, C), jnp.int32))
    block_on = block_s[r, duo]
    for s in range(16):
        col_chain = jnp.where(lane < 64, chain_s[c * 32 + s], chain_s[c * 32 + 16 + s])
        allowed = jnp.logical_or(row_chain == col_chain, block_on == 1)
        keep_0[s // 4 : s // 4 + 1, (s % 4) * 128 : (s % 4 + 1) * 128] = jnp.where(
            allowed, 1.0, 0.0
        ).astype(F32)

    wide[0:2048, :] = pair[...].astype(F32).reshape(2048, C)

    for a in range(4):
        for b in range(4):
            s = a * 4 + b
            x = jnp.concatenate(
                [wide[pl.ds(s, 64, stride=32), :], wide[pl.ds(16 + s, 64, stride=32), :]], axis=0
            )
            norm_0[a, :, b * 128 : (b + 1) * 128] = norm_cm(jnp.transpose(x), gain_b[0]).astype(
                BF16
            )

    for half in range(2):
        for step in (2 * half, 2 * half + 1):
            make_edges(0, step * 32, norm_0, keep_0)
        if half == 0:
            pl.semaphore_wait(barrier, DEV - 1)
        send_far(send_a.at[0], recv_a.at[0], 1, (half,))
    send_near(send_a.at[0], recv_a.at[0], 1)

    pltpu.make_async_copy(
        pair.at[:, place], rows_in.at[:, pl.ds(c * 32, 32)], sem_recv.at[0]
    ).start()

    @pl.loop(1, COLS)
    def _(step):
        t = lax.rem(c + step, COLS)
        pltpu.make_async_remote_copy(
            pair.at[:, lax.rem(t, 2) * 8 + lax.div(t, 2)],
            rows_in.at[:, pl.ds(c * 32, 32)],
            sem_send.at[0],
            sem_recv.at[0],
            device_id=(r, t),
            device_id_type=MESH,
        ).start()

    for n in range(1, 5):
        set_gain(n)
    set_in(1)
    for t in range(2):
        wt_out[t] = jnp.transpose(w_out[t].astype(F32)).astype(BF16)
    wt_k[...] = jnp.transpose(w_attn[:, C : 2 * C].astype(F32)).astype(BF16)

    block_of = lax.broadcasted_iota(jnp.int32, (1, N), 1) // 64
    linked = jnp.zeros((1, N), jnp.int32)
    for nb in range(8):
        linked = jnp.where(block_of == nb, block_s[r, nb], linked)
    for i in range(2 * OWN):
        at = place if i < OWN else other * 8 + duo
        own_chain = chain_s[r * 64 + (i % OWN) * 16 + at]
        allowed = jnp.logical_or(chain_v[...] == own_chain, linked == 1)
        keep8[i : i + 1, :] = jnp.where(allowed, 1.0, 0.0).astype(F32)

    def triangle(t, k):
        arrived(recv_a.at[t], k)
        if t == 0:
            low = lax.broadcasted_iota(jnp.int32, (C, C), 1) < 64
            for side in range(2):
                for q in range(4):
                    for k2 in range(2):
                        first = k2 * CHIPS + 2 * q * 8
                        here = recv_a[t, pl.ds(first, 8), side * 16 : side * 16 + 16]
                        there = recv_a[t, pl.ds(first + 8, 8), side * 16 : side * 16 + 16]
                        here = here.astype(F32).reshape(C, C)
                        there = there.astype(F32).reshape(C, C)
                        at = k2 * 128
                        edges[side, pl.ds(at, 128), q * 128 : (q + 1) * 128] = jnp.where(
                            low, here, pltpu.roll(there, 64, 1)
                        ).astype(BF16)
                        edges[side, pl.ds(at + 256, 128), q * 128 : (q + 1) * 128] = jnp.where(
                            low, pltpu.roll(here, 64, 1), there
                        ).astype(BF16)
        else:
            wide[...] = recv_a[t].astype(F32).reshape(4096, 128)
            for side in range(2):
                for b in range(4):
                    for a in range(OWN):
                        block = wide[pl.ds(side * 16 + a * 4 + b, 128, stride=32), :]
                        edges[
                            side, a * 128 : (a + 1) * 128, b * 128 : (b + 1) * 128
                        ] = block.astype(BF16)

        for q in range(4):
            left = edges[0, :, q * 128 : (q + 1) * 128]
            total = dot(jnp.transpose(left.astype(F32)).astype(BF16), edges[1])
            for half in range(2):
                for a in range(OWN):
                    for k2 in range(2):
                        for b in range(4):
                            at = (k2 * CHIPS + (2 * q + half) * 8) * 16 + a * 4 + b
                            row = half * 64 + a * 16 + k2 * 8
                            wide[pl.ds(at, 8, stride=16), :] = total[
                                row : row + 8, b * 128 : (b + 1) * 128
                            ]

        for k2 in range(2):
            part = wide[k2 * 1024 : (k2 + 1) * 1024, :].reshape(CHIPS, 16, 128)
            send_b[t, k2 * CHIPS : (k2 + 1) * CHIPS] = part.astype(BF16)
            send_far(send_b.at[t], recv_b.at[t], k + 1, (k2,))
        send_near(send_b.at[t], recv_b.at[t], k + 1)

    def gates(t):
        for a in range(OWN):
            gate_cm[a] = jax.nn.sigmoid(dot(wt_in[t, 4 * C : 5 * C, :], norm8[a]))

    def finish(t, k, then):
        arrived(recv_b.at[t], k)
        wide[0:2048, :] = recv_b[t].astype(F32).reshape(2048, 128)

        for a in range(OWN):
            total = jnp.concatenate(
                [wide[pl.ds(a * 4 + b, 128, stride=16), :] for b in range(4)], axis=1
            )
            normed = norm_cm(total, jnp.tile(gain_b[2 * t + 1], (1, 4))).astype(BF16)
            update = gate_cm[a] * dot(wt_out[t], normed)
            new = (pair_cm[a] + update).astype(BF16).astype(F32)
            pair_cm[a] = new
            then(a, norm_cm(new, jnp.tile(gain_b[2 * t + 2], (1, 4))).astype(BF16))

    triangle(0, 1)

    arrived(rows_in, 0)
    for a in range(OWN):
        x = jnp.transpose(rows_in[a].astype(F32))
        pair_cm[a] = x
        norm8[a] = norm_cm(x, jnp.tile(gain_b[0], (1, 4))).astype(BF16)

    gates(0)

    def keep_norm(a, normed):
        norm8[a] = normed

    finish(0, 2, keep_norm)

    for half in range(2):
        for step in (2 * half, 2 * half + 1):
            make_edges(1, step * 32, norm8, keep8)

        send_far(send_a.at[1], recv_a.at[1], 3, (half,))
    send_near(send_a.at[1], recv_a.at[1], 3)
    gates(1)
    triangle(1, 3)

    sibling = (r, duo * 2 + other)
    own_half = pl.multiple_of(core * HALF, HALF)

    def bias_part(a, normed):
        norm8[a] = normed
        bias = dot(w_bias[...], normed)
        for h in range(H):
            for kb in range(4):
                wide[pl.ds(2048 + h * 16 + kb * 4 + a, 1), :] = bias[
                    h : h + 1, kb * 128 : (kb + 1) * 128
                ]
        half_send[a] = pair_cm[a, :, pl.ds(pl.multiple_of(other * HALF, HALF), HALF)].astype(BF16)
        resid8[a] = pair_cm[a, :, pl.ds(own_half, HALF)].astype(BF16)
        for source, target, k in (
            (norm8.at[a], norm8.at[OWN + a], 6),
            (half_send.at[a], resid8.at[OWN + a], 7),
        ):
            pltpu.make_async_remote_copy(
                source,
                target,
                sem_send.at[k],
                sem_recv.at[k + 3],
                device_id=sibling,
                device_id_type=MESH,
            ).start()

    finish(1, 4, bias_part)
    bias_send[...] = wide[2048 : 2048 + 64, :].reshape(H, 16, 128).astype(BF16)

    asks = lax.div(r, 4)
    slot = cy * 16 + place

    def send_bias(h):
        def visit(r2, duo2):
            pltpu.make_async_remote_copy(
                bias_send.at[h],
                bias_recv.at[h, slot],
                sem_send.at[5],
                sem_recv.at[5 + h],
                device_id=(r2, duo2 * 2 + asks),
                device_id_type=MESH,
            ).start()

        far_chips(visit)

        @pl.when(asks == core)
        def _():
            pltpu.make_async_copy(
                bias_send.at[h], bias_recv.at[h, slot], sem_recv.at[5 + h]
            ).start()

        @pl.when(asks != core)
        def _():
            visit(r, duo)

    lane_q = lax.broadcasted_iota(jnp.int32, (HALF, C), 1)
    lane_v = lax.broadcasted_iota(jnp.int32, (N, C), 1)
    first_lane = jnp.where(lane_q == 0, 1.0, 0.0).astype(BF16)
    first_row = lax.broadcasted_iota(jnp.int32, (C, N), 0) == 0

    def prepare(i):
        k_ext[i, 0:C, :] = dot(wt_k[...], norm8[i]).astype(BF16)
        penalty = jnp.where(keep8[i : i + 1, :] > 0.5, 0.0, -1e9)
        k_ext[i, C:, :] = jnp.where(first_row, penalty, 0.0).astype(BF16)
        rows_in[0] = jnp.transpose(norm8[i].astype(F32)).astype(BF16)
        values = dot(rows_in[0], w_attn[:, 2 * C : 3 * C])
        asked = rows_in[0, pl.ds(own_half, HALF), :]
        queries = dot(asked, w_attn[:, 0:C]) * (32**-0.5 * LOG2E)
        gate8[i] = jax.nn.sigmoid(dot(asked, w_attn[:, 3 * C :]))
        for h in range(H):
            here_q = jnp.logical_and(lane_q >= 32 * h, lane_q < 32 * (h + 1))
            here_v = jnp.logical_and(lane_v >= 32 * h, lane_v < 32 * (h + 1))
            q_ext[i, h, :, 0:C] = jnp.where(here_q, queries, 0.0).astype(BF16)
            q_ext[i, h, :, C:] = first_lane
            v_ext[i, h, :, 0:C] = jnp.where(here_v, values, 0.0).astype(BF16)
            v_ext[i, h, :, C:] = jnp.ones((N, C), BF16)

    for h in range(H):
        send_bias(h)
        if h == 2:
            arrived(norm8.at[pl.ds(OWN, OWN)], 9)
        prepare(2 * h)
        prepare(2 * h + 1)
    arrived(resid8.at[pl.ds(OWN, OWN)], 10)

    def out_part(i, u):
        owner = (core if i < OWN else other) * 8 + duo
        return rows_out.at[i, pl.ds(pl.multiple_of(u * 32, 32), 32)], out.at[i % OWN, owner]

    def send_out(i, u):
        source, target = out_part(i, u)
        pltpu.make_async_remote_copy(
            source,
            target,
            sem_send.at[8],
            sem_recv.at[11],
            device_id=(r, core * 8 + u),
            device_id_type=MESH,
        ).start()

    for h in range(H):
        arrived(bias_recv.at[h], 5 + h)
        wide[0:1024, :] = bias_recv[h].astype(F32).reshape(1024, 128) * LOG2E
        for y in range(4):
            for a in range(OWN):
                for kb in range(4):
                    bias_nat[
                        y * 64 + a * 16 : y * 64 + a * 16 + 16, kb * 128 : (kb + 1) * 128
                    ] = wide[pl.ds(y * 256 + kb * 4 + a, 16, stride=16), :]

        for i in range(2 * OWN):
            scores = dot(q_ext[i, h], k_ext[i]) + bias_nat[...]
            mixed = dot(jnp.exp2(scores).astype(BF16), v_ext[i, h])
            part = mixed[:, 0:C] * inverse(mixed[:, C:])
            if h == 0:
                total8[i] = part
            elif h < H - 1:
                total8[i] += part
            else:
                gated = (gate8[i] * (total8[i] + part)).astype(BF16)
                update = dot(gated, w_final[...])
                rows_out[i] = (jnp.transpose(resid8[i].astype(F32)) + update).astype(BF16)
                for u in range(1, 8):
                    send_out(i, lax.rem(c + u, 8))

    @pl.when(lax.div(c, 8) == core)
    def _():
        for i in range(2 * OWN):
            source, target = out_part(i, lax.rem(c, 8))
            pltpu.make_async_copy(source, target, sem_recv.at[11]).start()

    @pl.when(lax.div(c, 8) != core)
    def _():
        for i in range(2 * OWN):
            send_out(i, lax.rem(c, 8))

    arrived(out, 11)

    sent(out.at[:, pl.ds(0, COLS - 1)], 0)
    for t in range(2):
        sent(recv_a.at[t, pl.ds(0, DEV - 1)], 2 * t + 1)
        sent(recv_b.at[t, pl.ds(0, DEV - 1)], 2 * t + 2)
    sent(norm8.at[pl.ds(0, OWN)], 6)
    sent(half_send, 7)

    @pl.when(asks == core)
    def _():
        sent(bias_recv.at[:, pl.ds(0, CHIPS - 1)], 5)

    @pl.when(asks != core)
    def _():
        sent(bias_recv, 5)

    @pl.when(lax.div(c, 8) == core)
    def _():
        sent(out.at[:, pl.ds(0, COLS - 2)], 8)

    @pl.when(lax.div(c, 8) != core)
    def _():
        sent(out, 8)


def per_device(
    pair, chain_id, block_mask, norm_gains, w_in, w_out, w_attn, w_bias, w_final
):
    vmem = pl.BlockSpec(memory_space=pltpu.VMEM)
    smem = pl.BlockSpec(memory_space=pltpu.SMEM)
    result = pl.pallas_call(
        kernel,
        out_shape=pltpu.VMEM((OWN, COLS, 32, C), BF16),
        in_specs=[vmem, smem, vmem, smem] + [vmem] * 6,
        out_specs=vmem,
        scratch_shapes=[
            pltpu.VMEM((OWN, N, C), BF16),
            pltpu.VMEM((OWN, C, N), F32),
            pltpu.VMEM((OWN, C, N), F32),
            pltpu.VMEM((2 * OWN, C, N), BF16),
            pltpu.VMEM((OWN, C, N), BF16),
            pltpu.VMEM((2 * OWN, N), F32),
            pltpu.VMEM((8, N), F32),
            pltpu.VMEM((5, C, C), F32),
            pltpu.VMEM((2, 5 * C, C), BF16),
            pltpu.VMEM((2, C, C), BF16),
            pltpu.VMEM((C, C), BF16),
            pltpu.VMEM((4096, C), F32),
            pltpu.VMEM((2, N, N), BF16),
            pltpu.VMEM((2, DEV, 32, C), BF16),
            pltpu.VMEM((2, DEV, 32, C), BF16),
            pltpu.VMEM((2, DEV, 16, C), BF16),
            pltpu.VMEM((2, DEV, 16, C), BF16),
            pltpu.VMEM((H, 16, C), BF16),
            pltpu.VMEM((H, CHIPS, 16, C), BF16),
            pltpu.VMEM((HALF, N), F32),
            pltpu.VMEM((OWN, C, HALF), BF16),
            pltpu.VMEM((2 * OWN, C, HALF), BF16),
            pltpu.VMEM((2 * OWN, H, HALF, 2 * C), BF16),
            pltpu.VMEM((2 * OWN, 2 * C, N), BF16),
            pltpu.VMEM((2 * OWN, H, N, 2 * C), BF16),
            pltpu.VMEM((2 * OWN, HALF, C), F32),
            pltpu.VMEM((2 * OWN, HALF, C), F32),
            pltpu.VMEM((2 * OWN, HALF, C), BF16),
            pltpu.SemaphoreType.DMA((9,)),
            pltpu.SemaphoreType.DMA((12,)),
        ],
        name="triangle_block",
        compiler_params=pltpu.CompilerParams(
            collective_id=0, has_side_effects=True, vmem_limit_bytes=60 << 20
        ),
        cost_estimate=pl.CostEstimate(
            flops=3 * 10**9, bytes_accessed=2 * 10**6, transcendentals=5 * 10**6
        ),
    )(
        pair.reshape(OWN, COLS, 32, C),
        chain_id,
        chain_id.reshape(1, N),
        block_mask,
        norm_gains,
        w_in,
        w_out,
        w_attn,
        w_bias.T,
        w_final,
    )
    return result.reshape(64, 32, C)


def solution(mesh):
    placed = (P("row", "col", None), P(), P(), P(), P(), P(), P(), P(), P())
    return jax.shard_map(
        per_device, mesh=mesh, in_specs=placed, out_specs=P("row", "col", None), check_vma=False
    )
```

```python
import jax
import jax.numpy as jnp
from jax import lax
from jax.experimental import pallas as pl
from jax.experimental.pallas import tpu as pltpu
from jax.sharding import PartitionSpec as P

MESH = pl.DeviceIdType.MESH
F32 = jnp.float32
BF16 = jnp.bfloat16
ROWS = 8
COLS = 16
DEV = ROWS * COLS
CHIPS = DEV // 2
C = 128
N = 512
HALF = N // 2
H = 4
OWN = 4
LOG2E = 1.4426950408889634

FAR = (
    (699248298, 5),
    (791255470, 5),
    (966748069, 5),
    (770581915, 5),
    (199256638, 5),
    (744454258, 5),
    (160421045, 5),
    (612196317, 5),
    (322204568, 5),
    (336278469, 5),
    (539184252, 5),
    (51578641, 5),
    (49232, 3),
)


def dot(a, b):
    return jnp.dot(a, b, preferred_element_type=F32)


def inverse(x):
    guess = pltpu.reciprocal(x, approx=True)
    return guess * (2.0 - x * guess)


def sigmoid(x):
    return 0.5 * jnp.tanh(0.5 * x) + 0.5


def norm_cm(x, gain):
    center = x - jnp.mean(x, axis=0, keepdims=True)
    spread = jnp.mean(center * center, axis=0, keepdims=True)
    return center * lax.rsqrt(spread + 1e-05) * gain


def kernel(
    pair,
    chain_s,
    chain_v,
    block_s,
    gains,
    w_in,
    w_out,
    w_attn,
    w_bias,
    w_final,
    out,
    rows_in,
    pair_cm,
    gate_cm,
    norm8,
    norm_0,
    keep8,
    keep_0,
    gain_b,
    wt_in,
    wt_out,
    wt_k,
    wide,
    edges,
    send_a,
    recv_a,
    send_b,
    recv_b,
    bias_send,
    bias_recv,
    bias_nat,
    half_send,
    resid8,
    q_ext,
    k_ext,
    v_ext,
    gate8,
    total8,
    rows_out,
    sem_send,
    sem_recv,
):
    r = lax.axis_index("row")
    c = lax.axis_index("col")
    core = lax.rem(c, 2)
    duo = lax.div(c, 2)
    chip = r * 8 + duo
    me = core * CHIPS + chip
    place = core * 8 + duo
    other = 1 - core
    cx = lax.rem(duo, 2) * 2 + lax.div(r, 4)
    cy = lax.rem(r, 4)
    cz = lax.div(duo, 2)

    barrier = pltpu.get_barrier_semaphore()

    def greet(i, j):
        pl.semaphore_signal(
            barrier,
            inc=1,
            device_id=(lax.rem(r + i, ROWS), lax.rem(c + j, COLS)),
            device_id_type=MESH,
        )

    for j in range(1, COLS):
        greet(0, j)

    for i in range(1, ROWS):
        for j in range(COLS):
            greet(i, j)

    def far_chips(visit):
        for packed, count in FAR:

            def body(_, value):
                d = lax.rem(value, 64)
                x = lax.rem(cx + lax.rem(d, 4), 4)
                y = lax.rem(cy + lax.rem(lax.div(d, 4), 4), 4)
                z = lax.rem(cz + lax.div(d, 16), 4)
                visit(lax.rem(x, 2) * 4 + y, z * 2 + lax.div(x, 2))
                return lax.div(value, 64)

            lax.fori_loop(0, count, body, jnp.int32(packed))

    def chunk(source, target, k, r2, duo2, core2):
        t = core2 * CHIPS + r2 * 8 + duo2
        pltpu.make_async_remote_copy(
            source.at[t],
            target.at[me],
            sem_send.at[k],
            sem_recv.at[k],
            device_id=(r2, duo2 * 2 + core2),
            device_id_type=MESH,
        ).start()

    def send_far(source, target, k, cores):
        def visit(r2, duo2):
            for core2 in cores:
                chunk(source, target, k, r2, duo2, core2)

        far_chips(visit)

    def send_near(source, target, k):
        pltpu.make_async_copy(source.at[me], target.at[me], sem_recv.at[k]).start()
        chunk(source, target, k, r, duo, other)

    def arrived(array, k):
        pltpu.make_async_copy(array, array, sem_recv.at[k]).wait()

    def sent(array, k):
        pltpu.make_async_copy(array, array, sem_send.at[k]).wait()

    def make_edges(t, base, normed, mask):
        for a in range(OWN):
            x = normed[a]
            m = mask[a : a + 1, :]
            for side in range(2):
                g = dot(wt_in[t, pl.ds(2 * side * C + base, 32), :], x)
                v = dot(wt_in[t, pl.ds((2 * side + 1) * C + base, 32), :], x)
                e = sigmoid(g) * v * m
                for b in range(4):
                    wide[pl.ds(base * 32 + side * 16 + a * 4 + b, 32, stride=32), :] = e[
                        :, b * 128 : (b + 1) * 128
                    ]
        part = wide[base * 32 : base * 32 + 1024, :]
        send_a[t, base : base + 32] = part.reshape(32, 32, 128).astype(BF16)

    def set_in(t):
        for g in range(5):
            part = w_in[t, :, g * C : (g + 1) * C].astype(F32)
            wt_in[t, g * C : (g + 1) * C, :] = jnp.transpose(part).astype(BF16)

    def set_gain(n):
        gain_b[n] = jnp.transpose(jnp.broadcast_to(gains[n : n + 1, :], (C, C)))

    set_in(0)
    set_gain(0)

    lane = lax.broadcasted_iota(jnp.int32, (1, C), 1)
    row_of = lax.rem(lane, 64)

    def pick(il, chains):
        return jnp.where(row_of == il, chain_s[r * 64 + il], chains)

    row_chain = lax.fori_loop(0, 64, pick, jnp.zeros((1, C), jnp.int32))
    block_on = block_s[r, duo]
    for s in range(16):
        col_chain = jnp.where(lane < 64, chain_s[c * 32 + s], chain_s[c * 32 + 16 + s])
        allowed = jnp.logical_or(row_chain == col_chain, block_on == 1)
        keep_0[s // 4 : s // 4 + 1, (s % 4) * 128 : (s % 4 + 1) * 128] = jnp.where(
            allowed, 1.0, 0.0
        ).astype(F32)

    wide[0:2048, :] = pair[...].astype(F32).reshape(2048, C)

    for a in range(4):
        for b in range(4):
            s = a * 4 + b
            x = jnp.concatenate(
                [wide[pl.ds(s, 64, stride=32), :], wide[pl.ds(16 + s, 64, stride=32), :]], axis=0
            )
            norm_0[a, :, b * 128 : (b + 1) * 128] = norm_cm(jnp.transpose(x), gain_b[0]).astype(
                BF16
            )

    for half in range(2):
        for step in (2 * half, 2 * half + 1):
            make_edges(0, step * 32, norm_0, keep_0)
        if half == 0:
            pl.semaphore_wait(barrier, DEV - 1)
        send_far(send_a.at[0], recv_a.at[0], 1, (half,))
    send_near(send_a.at[0], recv_a.at[0], 1)

    pltpu.make_async_copy(
        pair.at[:, place], rows_in.at[:, pl.ds(c * 32, 32)], sem_recv.at[0]
    ).start()

    @pl.loop(1, COLS)
    def _(step):
        t = lax.rem(c + step, COLS)
        pltpu.make_async_remote_copy(
            pair.at[:, lax.rem(t, 2) * 8 + lax.div(t, 2)],
            rows_in.at[:, pl.ds(c * 32, 32)],
            sem_send.at[0],
            sem_recv.at[0],
            device_id=(r, t),
            device_id_type=MESH,
        ).start()

    for n in range(1, 5):
        set_gain(n)
    set_in(1)
    for t in range(2):
        wt_out[t] = jnp.transpose(w_out[t].astype(F32)).astype(BF16)
    wt_k[...] = jnp.transpose(w_attn[:, C : 2 * C].astype(F32)).astype(BF16)

    block_of = lax.broadcasted_iota(jnp.int32, (1, N), 1) // 64
    linked = jnp.zeros((1, N), jnp.int32)
    for nb in range(8):
        linked = jnp.where(block_of == nb, block_s[r, nb], linked)
    for i in range(2 * OWN):
        at = place if i < OWN else other * 8 + duo
        own_chain = chain_s[r * 64 + (i % OWN) * 16 + at]
        allowed = jnp.logical_or(chain_v[...] == own_chain, linked == 1)
        keep8[i : i + 1, :] = jnp.where(allowed, 1.0, 0.0).astype(F32)

    def triangle(t, k):
        arrived(recv_a.at[t], k)
        if t == 0:
            low = lax.broadcasted_iota(jnp.int32, (C, C), 1) < 64
            for side in range(2):
                for q in range(4):
                    for k2 in range(2):
                        first = k2 * CHIPS + 2 * q * 8
                        here = recv_a[t, pl.ds(first, 8), side * 16 : side * 16 + 16]
                        there = recv_a[t, pl.ds(first + 8, 8), side * 16 : side * 16 + 16]
                        here = here.astype(F32).reshape(C, C)
                        there = there.astype(F32).reshape(C, C)
                        at = k2 * 128
                        edges[side, pl.ds(at, 128), q * 128 : (q + 1) * 128] = jnp.where(
                            low, here, pltpu.roll(there, 64, 1)
                        ).astype(BF16)
                        edges[side, pl.ds(at + 256, 128), q * 128 : (q + 1) * 128] = jnp.where(
                            low, pltpu.roll(here, 64, 1), there
                        ).astype(BF16)
        else:
            wide[...] = recv_a[t].astype(F32).reshape(4096, 128)
            for side in range(2):
                for b in range(4):
                    for a in range(OWN):
                        block = wide[pl.ds(side * 16 + a * 4 + b, 128, stride=32), :]
                        edges[
                            side, a * 128 : (a + 1) * 128, b * 128 : (b + 1) * 128
                        ] = block.astype(BF16)

        for q in range(4):
            left = edges[0, :, q * 128 : (q + 1) * 128]
            total = dot(jnp.transpose(left.astype(F32)).astype(BF16), edges[1])
            for half in range(2):
                for a in range(OWN):
                    for k2 in range(2):
                        for b in range(4):
                            at = (k2 * CHIPS + (2 * q + half) * 8) * 16 + a * 4 + b
                            row = half * 64 + a * 16 + k2 * 8
                            wide[pl.ds(at, 8, stride=16), :] = total[
                                row : row + 8, b * 128 : (b + 1) * 128
                            ]

        for k2 in range(2):
            part = wide[k2 * 1024 : (k2 + 1) * 1024, :].reshape(CHIPS, 16, 128)
            send_b[t, k2 * CHIPS : (k2 + 1) * CHIPS] = part.astype(BF16)
            send_far(send_b.at[t], recv_b.at[t], k + 1, (k2,))
        send_near(send_b.at[t], recv_b.at[t], k + 1)

    def gates(t):
        for a in range(OWN):
            gate_cm[a] = sigmoid(dot(wt_in[t, 4 * C : 5 * C, :], norm8[a]))

    def finish(t, k, then):
        arrived(recv_b.at[t], k)
        wide[0:2048, :] = recv_b[t].astype(F32).reshape(2048, 128)

        for a in range(OWN):
            total = jnp.concatenate(
                [wide[pl.ds(a * 4 + b, 128, stride=16), :] for b in range(4)], axis=1
            )
            normed = norm_cm(total, jnp.tile(gain_b[2 * t + 1], (1, 4))).astype(BF16)
            update = gate_cm[a] * dot(wt_out[t], normed)
            new = (pair_cm[a] + update).astype(BF16).astype(F32)
            pair_cm[a] = new
            then(a, norm_cm(new, jnp.tile(gain_b[2 * t + 2], (1, 4))).astype(BF16))

    triangle(0, 1)

    arrived(rows_in, 0)
    for a in range(OWN):
        x = jnp.transpose(rows_in[a].astype(F32))
        pair_cm[a] = x
        norm8[a] = norm_cm(x, jnp.tile(gain_b[0], (1, 4))).astype(BF16)

    gates(0)

    def keep_norm(a, normed):
        norm8[a] = normed

    finish(0, 2, keep_norm)

    for half in range(2):
        for step in (2 * half, 2 * half + 1):
            make_edges(1, step * 32, norm8, keep8)

        send_far(send_a.at[1], recv_a.at[1], 3, (half,))
    send_near(send_a.at[1], recv_a.at[1], 3)
    gates(1)
    triangle(1, 3)

    sibling = (r, duo * 2 + other)
    own_half = pl.multiple_of(core * HALF, HALF)

    def bias_part(a, normed):
        norm8[a] = normed
        bias = dot(w_bias[...], normed)
        for h in range(H):
            for kb in range(4):
                wide[pl.ds(2048 + h * 16 + kb * 4 + a, 1), :] = bias[
                    h : h + 1, kb * 128 : (kb + 1) * 128
                ]
        half_send[a] = pair_cm[a, :, pl.ds(pl.multiple_of(other * HALF, HALF), HALF)].astype(BF16)
        resid8[a] = pair_cm[a, :, pl.ds(own_half, HALF)].astype(BF16)

    finish(1, 4, bias_part)
    for source, target, k in (
        (norm8.at[pl.ds(0, OWN)], norm8.at[pl.ds(OWN, OWN)], 6),
        (half_send, resid8.at[pl.ds(OWN, OWN)], 7),
    ):
        pltpu.make_async_remote_copy(
            source,
            target,
            sem_send.at[k],
            sem_recv.at[k + 3],
            device_id=sibling,
            device_id_type=MESH,
        ).start()
    bias_send[...] = wide[2048 : 2048 + 64, :].reshape(H, 16, 128).astype(BF16)

    asks = lax.div(r, 4)
    slot = cy * 16 + place

    def send_bias(h):
        def visit(r2, duo2):
            pltpu.make_async_remote_copy(
                bias_send.at[h],
                bias_recv.at[h, slot],
                sem_send.at[5],
                sem_recv.at[5 + h],
                device_id=(r2, duo2 * 2 + asks),
                device_id_type=MESH,
            ).start()

        far_chips(visit)

        @pl.when(asks == core)
        def _():
            pltpu.make_async_copy(
                bias_send.at[h], bias_recv.at[h, slot], sem_recv.at[5 + h]
            ).start()

        @pl.when(asks != core)
        def _():
            visit(r, duo)

    lane_q = lax.broadcasted_iota(jnp.int32, (HALF, C), 1)
    lane_v = lax.broadcasted_iota(jnp.int32, (N, C), 1)
    first_lane = jnp.where(lane_q == 0, 1.0, 0.0).astype(BF16)
    first_row = lax.broadcasted_iota(jnp.int32, (C, N), 0) == 0

    def prepare(i):
        k_ext[i, 0:C, :] = dot(wt_k[...], norm8[i]).astype(BF16)
        penalty = jnp.where(keep8[i : i + 1, :] > 0.5, 0.0, -1e9)
        k_ext[i, C:, :] = jnp.where(first_row, penalty, 0.0).astype(BF16)
        rows_in[0] = jnp.transpose(norm8[i].astype(F32)).astype(BF16)
        values = dot(rows_in[0], w_attn[:, 2 * C : 3 * C])
        asked = rows_in[0, pl.ds(own_half, HALF), :]
        queries = dot(asked, w_attn[:, 0:C]) * (32**-0.5 * LOG2E)
        gate8[i] = sigmoid(dot(asked, w_attn[:, 3 * C :]))
        for h in range(H):
            here_q = jnp.logical_and(lane_q >= 32 * h, lane_q < 32 * (h + 1))
            here_v = jnp.logical_and(lane_v >= 32 * h, lane_v < 32 * (h + 1))
            q_ext[i, h, :, 0:C] = jnp.where(here_q, queries, 0.0).astype(BF16)
            q_ext[i, h, :, C:] = first_lane
            v_ext[i, h, :, 0:C] = jnp.where(here_v, values, 0.0).astype(BF16)
            v_ext[i, h, :, C:] = jnp.ones((N, C), BF16)

    for h in range(H):
        send_bias(h)
        if h == 2:
            arrived(norm8.at[pl.ds(OWN, OWN)], 9)
        prepare(2 * h)
        prepare(2 * h + 1)
    arrived(resid8.at[pl.ds(OWN, OWN)], 10)

    def out_part(i, u):
        owner = (core if i < OWN else other) * 8 + duo
        return rows_out.at[i, pl.ds(pl.multiple_of(u * 32, 32), 32)], out.at[i % OWN, owner]

    def send_out(i, u):
        source, target = out_part(i, u)
        pltpu.make_async_remote_copy(
            source,
            target,
            sem_send.at[8],
            sem_recv.at[11],
            device_id=(r, core * 8 + u),
            device_id_type=MESH,
        ).start()

    for h in range(H):
        arrived(bias_recv.at[h], 5 + h)
        wide[0:1024, :] = bias_recv[h].astype(F32).reshape(1024, 128) * LOG2E
        for y in range(4):
            for a in range(OWN):
                for kb in range(4):
                    bias_nat[
                        y * 64 + a * 16 : y * 64 + a * 16 + 16, kb * 128 : (kb + 1) * 128
                    ] = wide[pl.ds(y * 256 + kb * 4 + a, 16, stride=16), :]

        for i in range(2 * OWN):
            scores = dot(q_ext[i, h], k_ext[i]) + bias_nat[...]
            mixed = dot(jnp.exp2(scores).astype(BF16), v_ext[i, h])
            part = mixed[:, 0:C] * inverse(mixed[:, C:])
            if h == 0:
                total8[i] = part
            elif h < H - 1:
                total8[i] += part
            else:
                gated = (gate8[i] * (total8[i] + part)).astype(BF16)
                update = dot(gated, w_final[...])
                rows_out[i] = (jnp.transpose(resid8[i].astype(F32)) + update).astype(BF16)
                if i % 2 == 1:
                    for row in range(i - 1, i + 1):
                        for u in range(1, 8):
                            send_out(row, lax.rem(c + u, 8))

    @pl.when(lax.div(c, 8) == core)
    def _():
        for i in range(2 * OWN):
            source, target = out_part(i, lax.rem(c, 8))
            pltpu.make_async_copy(source, target, sem_recv.at[11]).start()

    @pl.when(lax.div(c, 8) != core)
    def _():
        for i in range(2 * OWN):
            send_out(i, lax.rem(c, 8))

    arrived(out, 11)

    sent(out.at[:, pl.ds(0, COLS - 1)], 0)
    for t in range(2):
        sent(recv_a.at[t, pl.ds(0, DEV - 1)], 2 * t + 1)
        sent(recv_b.at[t, pl.ds(0, DEV - 1)], 2 * t + 2)
    sent(norm8.at[pl.ds(0, OWN)], 6)
    sent(half_send, 7)

    @pl.when(asks == core)
    def _():
        sent(bias_recv.at[:, pl.ds(0, CHIPS - 1)], 5)

    @pl.when(asks != core)
    def _():
        sent(bias_recv, 5)

    @pl.when(lax.div(c, 8) == core)
    def _():
        sent(out.at[:, pl.ds(0, COLS - 2)], 8)

    @pl.when(lax.div(c, 8) != core)
    def _():
        sent(out, 8)


def per_device(
    pair, chain_id, block_mask, norm_gains, w_in, w_out, w_attn, w_bias, w_final
):
    vmem = pl.BlockSpec(memory_space=pltpu.VMEM)
    smem = pl.BlockSpec(memory_space=pltpu.SMEM)
    result = pl.pallas_call(
        kernel,
        out_shape=pltpu.VMEM((OWN, COLS, 32, C), BF16),
        in_specs=[vmem, smem, vmem, smem] + [vmem] * 6,
        out_specs=vmem,
        scratch_shapes=[
            pltpu.VMEM((OWN, N, C), BF16),
            pltpu.VMEM((OWN, C, N), F32),
            pltpu.VMEM((OWN, C, N), F32),
            pltpu.VMEM((2 * OWN, C, N), BF16),
            pltpu.VMEM((OWN, C, N), BF16),
            pltpu.VMEM((2 * OWN, N), F32),
            pltpu.VMEM((8, N), F32),
            pltpu.VMEM((5, C, C), F32),
            pltpu.VMEM((2, 5 * C, C), BF16),
            pltpu.VMEM((2, C, C), BF16),
            pltpu.VMEM((C, C), BF16),
            pltpu.VMEM((4096, C), F32),
            pltpu.VMEM((2, N, N), BF16),
            pltpu.VMEM((2, DEV, 32, C), BF16),
            pltpu.VMEM((2, DEV, 32, C), BF16),
            pltpu.VMEM((2, DEV, 16, C), BF16),
            pltpu.VMEM((2, DEV, 16, C), BF16),
            pltpu.VMEM((H, 16, C), BF16),
            pltpu.VMEM((H, CHIPS, 16, C), BF16),
            pltpu.VMEM((HALF, N), F32),
            pltpu.VMEM((OWN, C, HALF), BF16),
            pltpu.VMEM((2 * OWN, C, HALF), BF16),
            pltpu.VMEM((2 * OWN, H, HALF, 2 * C), BF16),
            pltpu.VMEM((2 * OWN, 2 * C, N), BF16),
            pltpu.VMEM((2 * OWN, H, N, 2 * C), BF16),
            pltpu.VMEM((2 * OWN, HALF, C), F32),
            pltpu.VMEM((2 * OWN, HALF, C), F32),
            pltpu.VMEM((2 * OWN, HALF, C), BF16),
            pltpu.SemaphoreType.DMA((9,)),
            pltpu.SemaphoreType.DMA((12,)),
        ],
        name="triangle_block",
        compiler_params=pltpu.CompilerParams(
            collective_id=0, has_side_effects=True, vmem_limit_bytes=60 << 20
        ),
        cost_estimate=pl.CostEstimate(
            flops=3 * 10**9, bytes_accessed=2 * 10**6, transcendentals=5 * 10**6
        ),
    )(
        pair.reshape(OWN, COLS, 32, C),
        chain_id,
        chain_id.reshape(1, N),
        block_mask,
        norm_gains,
        w_in,
        w_out,
        w_attn,
        w_bias.T,
        w_final,
    )
    return result.reshape(64, 32, C)


def solution(mesh):
    placed = (P("row", "col", None), P(), P(), P(), P(), P(), P(), P(), P())
    return jax.shard_map(
        per_device, mesh=mesh, in_specs=placed, out_specs=P("row", "col", None), check_vma=False
    )
```
